32 devices in a mesh: ax: 8 (over y, x, core), circ: 4 (over z).
Axes of the slice: x: 2, y: 2, z: 4, core: 2. Of those that a mesh axis runs over, the one named last changes fastest.
Arguments:
- endothelium: float32 [3, 32, 512, 128], P(None, 'ax', 'circ'), may hold values from -6 to 6
- muscle: float32 [3, 64, 256, 128], P(None, 'ax', 'circ'), may hold values from -6 to 6
- agonist: float32 [32, 512, 128], P('ax', 'circ'), may hold values from 0.2 to 2
- proj_cell: int32 [32, 32, 2], P(('ax', 'circ')), may hold values from 0 to 511
- proj_target: int32 [32, 32, 2], P(('ax', 'circ')), may hold values from 0 to 511
- proj_count: int32 [32, 32], P(('ax', 'circ')), may hold values from 0 to 2, as said below
- endo_inverse: float32 [3, 128, 128], replicated, may hold values from 0 to 0.29
- muscle_inverse: float32 [3, 128, 128], replicated, may hold values from 0 to 0.43
Outputs:
- endo_next: float32 [3, 32, 512, 128], P(None, 'ax', 'circ')
- muscle_next: float32 [3, 64, 256, 128], P(None, 'ax', 'circ')
The draws below stay inside these ranges and needn't reach their ends.
Inputs may be any that keep to these rules, and one draw needn't show every extreme that they name: `proj_count`: the live slots of a pair are its first ones. In every draw some owner receives 2 from every device and some device sends 2 to every owner.
All inputs are finite; a program needn't handle non-finite values.
Results may differ from the reference program's by a relative error of at most 0.0001.
Values sent between devices are 32-bit elements; how exact they have to be, the bound alone decides.
A program may use at most 64 MiB of HBM per device.

```python
import math
import jax
import jax.numpy as jnp
from jax import lax

POINTS = 128
ENDO_AX = 4
ENDO_CIRC = 128
MUSC_AX = 8
MUSC_CIRC = 64
PAIR_SLOTS = 2
TIME_STEPS = 8
OWNERS = 32
ENDO_CELLS = 512
MUSC_CELLS = 512
ENDO_LEN = 32
ENDO_CYCLE = 512
MUSC_LEN = 64
MUSC_CYCLE = 256


def cable_inverse(key, lengths, spread):
    index = jnp.arange(POINTS, dtype=jnp.float32)
    distance = jnp.abs(index[:, None] - index[None, :])
    length_scale = jnp.array(lengths, jnp.float32)[:, None, None]
    ratio = jnp.exp(-1.0 / length_scale)
    total = (1.0 + ratio) / (1.0 - ratio)
    rough = jax.random.uniform(key, (3, POINTS, POINTS), jnp.float32, 1.0 - spread, 1.0 + spread)
    return (jnp.exp(-distance[None] / length_scale) * rough / total).astype(jnp.float32)


def draw_endo_inverse(key, part):
    key = jax.random.fold_in(key, 11)
    return cable_inverse(key, [3.0, 8.0, 24.0], 0.5)


def draw_muscle_inverse(key, part):
    key = jax.random.fold_in(key, 13)
    return cable_inverse(key, [2.0, 6.0, 16.0], 0.5)


def draw_proj_count(key, part):
    key = jax.random.fold_in(key, 7)
    first, second, third = jax.random.split(key, 3)
    base = jax.random.randint(first, (OWNERS, OWNERS), 0, PAIR_SLOTS + 1, dtype=jnp.int32)
    sender = jax.random.randint(second, (), 0, OWNERS, dtype=jnp.int32)
    receiver = jax.random.randint(third, (), 0, OWNERS, dtype=jnp.int32)
    owner_ids = jnp.arange(OWNERS, dtype=jnp.int32)
    filled = (owner_ids[:, None] == sender) | (owner_ids[None, :] == receiver)
    return jnp.where(filled, PAIR_SLOTS, base).astype(jnp.int32)


def with_ends(values, stream_key, low, largest):
    dims = values.shape
    place = [jax.random.randint(jax.random.fold_in(stream_key, axis), (), 0, dims[axis]) for axis in range(len(dims))]
    values = values.at[tuple(place)].set(low)
    longest = dims.index(max(dims))
    place[longest] = (place[longest] + 1) % dims[longest]
    return values.at[tuple(place)].set(largest)


def shard_levels(rng, extent, shards, least, high):
    def one(axis_at, parts):
        draws = jax.random.uniform(jax.random.fold_in(jax.random.fold_in(rng, 6), axis_at), (parts,), jnp.float32, least / len(shards), high / len(shards))
        return jnp.repeat(jnp.exp(draws), extent[axis_at] // parts).reshape((-1,) + (1,) * (len(extent) - axis_at - 1))

    level = one(*shards[0])
    for cut in shards[1:]:
        level = level * one(*cut)
    return level


def normal_values(key, dims, width, limit, shards=(), kind=jnp.bfloat16):
    values = width * jax.random.normal(key, dims, jnp.float32)
    if shards:
        values = values * shard_levels(key, dims, shards, -0.22, 0.18)
    return jnp.clip(values, -limit, limit).astype(kind)


def setup_inputs(seed: int = 0) -> dict:
    splits = jax.random.split(jax.random.key(seed), 9)
    return {
        "endothelium": normal_values(splits[0], (3, ENDO_LEN, ENDO_CYCLE, POINTS), 1.0, 6.0, ((1, 8), (2, 4)), jnp.float32),
        "muscle": normal_values(splits[1], (3, MUSC_LEN, MUSC_CYCLE, POINTS), 1.0, 6.0, ((1, 8), (2, 4)), jnp.float32),
        "agonist": jnp.clip(jnp.exp(math.log(2.0) - 2.3025851 * jax.random.uniform(splits[2], (ENDO_LEN, ENDO_CYCLE, POINTS), jnp.float32) ** shard_levels(splits[2], (ENDO_LEN, ENDO_CYCLE, POINTS), ((0, 8), (1, 4)), -0.2, 0.2)), 0.2, 2.0),
        "proj_cell": with_ends(jax.random.randint(splits[3], (OWNERS, OWNERS, PAIR_SLOTS), 0, ENDO_CELLS), jax.random.fold_in(splits[3], 1), 0, ENDO_CELLS - 1).astype(jnp.int32),
        "proj_target": with_ends(jax.random.randint(splits[4], (OWNERS, OWNERS, PAIR_SLOTS), 0, MUSC_CELLS), jax.random.fold_in(splits[4], 1), 0, MUSC_CELLS - 1).astype(jnp.int32),
        "proj_count": draw_proj_count(jax.random.fold_in(splits[8], 71), 0),
        "endo_inverse": draw_endo_inverse(jax.random.fold_in(splits[8], 71), 0),
        "muscle_inverse": draw_muscle_inverse(jax.random.fold_in(splits[8], 71), 0),
    }


time_step = 0.2


def reaction(current, stimulus):
    calcium = current[0]
    inositol = current[1]
    voltage = current[2]
    release = inositol * inositol / (0.5 + inositol * inositol)
    return jnp.stack([1.2 * release - 0.6 * calcium - 0.2 * voltage,
                      stimulus - 0.5 * inositol,
                      0.5 * calcium - 0.8 * voltage])


def owner_rows(field, tile_axial, tile_cycle):
    species, length, cycle, points = field.shape
    blocks = field.reshape(species, length // tile_axial, tile_axial, cycle // tile_cycle, tile_cycle, points)
    return blocks.transpose(0, 1, 3, 2, 4, 5).reshape(species, -1, points)


def field_rows(rows, length, cycle, tile_axial, tile_cycle):
    species = rows.shape[0]
    points = rows.shape[2]
    blocks = rows.reshape(species, length // tile_axial, cycle // tile_cycle, tile_axial, tile_cycle, points)
    return blocks.transpose(0, 1, 3, 2, 4, 5).reshape(species, length, cycle, points)


def reference(endothelium, muscle, agonist, proj_cell, proj_target, proj_count, endo_inverse, muscle_inverse):
    owner_ids = jnp.arange(OWNERS, dtype=jnp.int32)
    endo_index = (owner_ids[:, None, None] * ENDO_CELLS + proj_cell).reshape(-1)
    muscle_index = (owner_ids[None, :, None] * MUSC_CELLS + proj_target).reshape(-1)
    slot_ids = jnp.arange(PAIR_SLOTS, dtype=jnp.int32)
    live_slot = (slot_ids[None, None, :] < proj_count[:, :, None]).astype(jnp.float32).reshape(-1)[None, :, None]
    coupling = jnp.array([0.1, 0.3, 0.5], jnp.float32)[:, None, None]
    endo_gap = jnp.array([0.05, 0.3, 0.5], jnp.float32)[:, None, None, None]
    muscle_gap = jnp.array([0.05, 0.1, 0.4], jnp.float32)[:, None, None, None]
    current_endo = endothelium
    current_muscle = muscle
    for step_index in range(TIME_STEPS):
        endo_rows = owner_rows(current_endo, ENDO_AX, ENDO_CIRC)
        muscle_rows = owner_rows(current_muscle, MUSC_AX, MUSC_CIRC)
        flux = coupling * (endo_rows[:, endo_index] - muscle_rows[:, muscle_index]) * live_slot
        endo_gain = field_rows(jnp.zeros_like(endo_rows).at[:, endo_index].add(-flux), ENDO_LEN, ENDO_CYCLE, ENDO_AX, ENDO_CIRC)
        muscle_gain = field_rows(jnp.zeros_like(muscle_rows).at[:, muscle_index].add(flux), MUSC_LEN, MUSC_CYCLE, MUSC_AX, MUSC_CIRC)
        endo_pad = jnp.pad(current_endo, ((0, 0), (1, 1), (0, 0), (0, 0)))
        endo_lap = endo_pad[:, 2:] + endo_pad[:, :-2] - 2.0 * current_endo
        muscle_lap = jnp.roll(current_muscle, 1, axis=2) + jnp.roll(current_muscle, -1, axis=2) - 2.0 * current_muscle
        endo_rhs = current_endo + time_step * (reaction(current_endo, agonist) + endo_gap * endo_lap + endo_gain)
        muscle_rhs = current_muscle + time_step * (reaction(current_muscle, 0.0) + muscle_gap * muscle_lap + muscle_gain)
        current_endo = jnp.einsum("sawj,sij->sawi", endo_rhs, endo_inverse, precision=lax.Precision.HIGHEST)
        current_muscle = jnp.einsum("sawj,sij->sawi", muscle_rhs, muscle_inverse, precision=lax.Precision.HIGHEST)
    return current_endo, current_muscle
```

```python
import functools

import jax
import jax.numpy as jnp
from jax import lax
from jax.experimental import pallas as pl
from jax.experimental.pallas import tpu as pltpu
from jax.sharding import PartitionSpec as P

MESH = pl.DeviceIdType.MESH
TIME_STEPS = 8
DT = 0.2
COUPLING = (0.1, 0.3, 0.5)
ENDO_GAP = (0.05, 0.3, 0.5)
MUSC_GAP = (0.05, 0.1, 0.4)
BF16 = jnp.bfloat16
F32 = jnp.float32


def halves(x):
    high = x.astype(BF16)
    return high, (x - high.astype(F32)).astype(BF16)


def side_by_side(x):
    return jnp.concatenate(halves(x), axis=1)


def folded(y):
    half = y.shape[1] // 2
    return y[:, :half] + y[:, half:]


def dot(a, b):
    return jnp.dot(a, b, preferred_element_type=F32)


def reaction(u0, u1, u2, drive):
    square = u1 * u1
    release = square / (0.5 + square)
    second = -0.5 * u1 if drive is None else drive - 0.5 * u1
    return (1.2 * release - 0.6 * u0 - 0.2 * u2, second, 0.5 * u0 - 0.8 * u2)


def kernel(
    sizes,
    endo_in, musc_in, agonist, endo_col, endo_row, musc_col, musc_row, endo_inv, musc_inv,
    endo_out, musc_out,
    endo, musc, halo_low, halo_high, edge_out, edge_left, edge_right,
    send, recv, picked, weights, take_e, take_m, put_e, put_m, rhs,
    in_sems, own_sem, send_sem, recv_sem, halo_send, halo_recv, edge_send, edge_recv,
):
    n_ax, n_circ, width, length, cycle = sizes
    n = n_ax * n_circ
    points = endo.shape[3]
    rows = endo.shape[2]
    musc_rows = musc.shape[2]
    ax = lax.axis_index("ax")
    circ = lax.axis_index("circ")
    me = ax * n_circ + circ
    right = lax.rem(circ + 1, n_circ)
    left = lax.rem(circ + n_circ - 1, n_circ)

    def place(p):
        return (p // n_circ, lax.rem(p, n_circ))

    load_e = pltpu.make_async_copy(endo_in, endo.at[0], in_sems.at[0])
    load_m = pltpu.make_async_copy(musc_in, musc.at[0], in_sems.at[1])
    load_e.start()
    load_m.start()

    barrier = pltpu.get_barrier_semaphore()

    def greet(k, carry):
        p = lax.rem(me + k, n)
        pl.semaphore_signal(barrier, inc=1, device_id=place(p), device_id_type=MESH)
        return carry

    lax.fori_loop(1, n, greet, 0)

    for layer, inv in ((0, endo_inv), (1, musc_inv)):
        for s in range(3):
            row = side_by_side(inv[s].T)
            weights[layer * 3 + s] = jnp.concatenate([row, row], axis=0)
    for col, row, take, put, count in (
        (endo_col, endo_row, take_e, put_e, rows), (musc_col, musc_row, take_m, put_m, musc_rows),
    ):
        ids = lax.broadcasted_iota(jnp.int32, take.shape, 1)
        take[...] = jnp.where(ids == col[...], 1.0, 0.0).astype(BF16)
        ids = lax.broadcasted_iota(jnp.int32, put.shape, 0)
        put[...] = jnp.where(ids == row[...], 1.0, 0.0).astype(BF16)

    @pl.when(ax == 0)
    def _():
        halo_low[...] = jnp.zeros_like(halo_low)

    @pl.when(ax == n_ax - 1)
    def _():
        halo_high[...] = jnp.zeros_like(halo_high)

    load_e.wait()
    load_m.wait()
    pl.semaphore_wait(barrier, n - 1)

    def step(t, carry):
        par = lax.rem(t, 2)
        nxt = 1 - par

        def to(p):
            return pltpu.make_async_remote_copy(
                src_ref=send.at[p, pl.ds(0, 12)],
                dst_ref=recv.at[par, me, pl.ds(0, 12)],
                send_sem=send_sem,
                recv_sem=recv_sem.at[par],
                device_id=place(p),
                device_id_type=MESH,
            )

        low = pltpu.make_async_remote_copy(
            src_ref=endo.at[par, :, pl.ds(0, width)], dst_ref=halo_high.at[par],
            send_sem=halo_send.at[0], recv_sem=halo_recv.at[par, 0],
            device_id=(ax - 1, circ), device_id_type=MESH,
        )
        high = pltpu.make_async_remote_copy(
            src_ref=endo.at[par, :, pl.ds(rows - width, width)], dst_ref=halo_low.at[par],
            send_sem=halo_send.at[1], recv_sem=halo_recv.at[par, 1],
            device_id=(ax + 1, circ), device_id_type=MESH,
        )
        to_left = pltpu.make_async_remote_copy(
            src_ref=edge_out.at[0], dst_ref=edge_right.at[par],
            send_sem=edge_send.at[0], recv_sem=edge_recv.at[par, 0],
            device_id=(ax, left), device_id_type=MESH,
        )
        to_right = pltpu.make_async_remote_copy(
            src_ref=edge_out.at[1], dst_ref=edge_left.at[par],
            send_sem=edge_send.at[1], recv_sem=edge_recv.at[par, 1],
            device_id=(ax, right), device_id_type=MESH,
        )

        flat = send.reshape(n * 16, points)
        for layer, state, take in ((0, endo, take_e), (1, musc, take_m)):
            for s in range(3):
                got = folded(dot(take[...], side_by_side(state[par, s])))
                picked[layer * 3 + s] = got
                for slot in range(2):
                    k = layer * 6 + s * 2 + slot
                    flat[pl.ds(k, n, stride=16), :] = got[slot * n:(slot + 1) * n]
        for s in range(3):
            edge_out[0, pl.ds(s * length, length)] = musc[par, s, pl.ds(0, length, stride=cycle), :]
            edge_out[1, pl.ds(s * length, length)] = musc[
                par, s, pl.ds(cycle - 1, length, stride=cycle), :
            ]

        @pl.when(ax > 0)
        def _():
            low.start()

        @pl.when(ax < n_ax - 1)
        def _():
            high.start()

        def launch(k, carry):
            to(lax.rem(me + k, n)).start()
            return carry

        lax.fori_loop(1, n, launch, 0)
        to_left.start()
        to_right.start()
        own = pltpu.make_async_copy(
            send.at[me, pl.ds(0, 12)], recv.at[par, me, pl.ds(0, 12)], own_sem
        )
        own.start()

        count = rows // width
        for a in range(count):
            for j in range(0, width, 64):
                here = pl.ds(a * width + j, 64)
                u = [endo[par, s, here, :] for s in range(3)]
                parts = reaction(u[0], u[1], u[2], agonist[here, :])
                for s in range(3):
                    lap = -2.0 * u[s]
                    if a > 0:
                        lap = lap + endo[par, s, pl.ds((a - 1) * width + j, 64), :]
                    if a < count - 1:
                        lap = lap + endo[par, s, pl.ds((a + 1) * width + j, 64), :]
                    value = u[s] + DT * (parts[s] + ENDO_GAP[s] * lap)
                    rhs[s, here, :] = side_by_side(value)

        def musc_base(a, carry):
            here = pl.ds(pl.multiple_of(a * cycle, cycle), cycle)
            place_in = lax.broadcasted_iota(jnp.int32, (cycle, points), 0)
            u = [musc[par, s, here, :] for s in range(3)]
            parts = reaction(u[0], u[1], u[2], None)
            for s in range(3):
                before = jnp.where(place_in == 0, 0.0, pltpu.roll(u[s], 1, 0))
                after = jnp.where(place_in == cycle - 1, 0.0, pltpu.roll(u[s], cycle - 1, 0))
                lap = before + after - 2.0 * u[s]
                value = u[s] + DT * (parts[s] + MUSC_GAP[s] * lap)
                rhs[3 + s, here, :] = side_by_side(value)
            return carry

        lax.fori_loop(0, length, musc_base, 0)

        for s in range(3):
            endo[nxt, s] = folded(dot(rhs[s], weights[s]))
            musc[nxt, s] = folded(dot(rhs[3 + s], weights[3 + s]))

        own.wait()
        every = pltpu.make_async_remote_copy(
            src_ref=send.at[pl.ds(0, n - 1), pl.ds(0, 12)],
            dst_ref=recv.at[par, pl.ds(0, n - 1), pl.ds(0, 12)],
            send_sem=send_sem, recv_sem=recv_sem.at[par],
            device_id=(ax, right), device_id_type=MESH,
        )
        every.wait_recv()
        to_left.wait_recv()
        to_right.wait_recv()

        @pl.when(ax > 0)
        def _():
            high.wait_recv()

        @pl.when(ax < n_ax - 1)
        def _():
            low.wait_recv()

        def arrived(layer, s):
            flat_in = recv.at[par].reshape(n * 16, points)
            k = layer * 6 + s * 2
            return jnp.concatenate(
                [flat_in[pl.ds(k + slot, n, stride=16), :] for slot in range(2)], axis=0
            )

        endo_flux, musc_flux, lows, highs, lefts, rights = [], [], [], [], [], []
        for s in range(3):
            flux = (DT * COUPLING[s]) * (arrived(1, s) - picked[s])
            gap = DT * ENDO_GAP[s]
            block = jnp.concatenate([gap * halo_low[par, s], gap * halo_high[par, s], flux], axis=0)
            block = folded(dot(side_by_side(block), weights[s]))
            lows.append(block[:width])
            highs.append(block[width:2 * width])
            endo_flux.append(block[2 * width:])
            flux = (DT * COUPLING[s]) * (arrived(0, s) - picked[3 + s])
            gap = DT * MUSC_GAP[s]
            span = pl.ds(s * length, length)
            block = jnp.concatenate(
                [gap * edge_left[par, span, :], gap * edge_right[par, span, :], flux], axis=0
            )
            block = folded(dot(side_by_side(block), weights[3 + s]))
            lefts.append(block[:length])
            rights.append(block[length:2 * length])
            musc_flux.append(block[2 * length:])

        for state, put, flux in ((endo, put_e, endo_flux), (musc, put_m, musc_flux)):
            stacked = jnp.concatenate(halves(jnp.concatenate(flux, axis=1)), axis=0)
            gain = dot(put[...], stacked)
            for s in range(3):
                state[nxt, s] = state[nxt, s] + gain[:, s * points:(s + 1) * points]
        for s in range(3):
            endo[nxt, s, pl.ds(0, width), :] += lows[s]
            endo[nxt, s, pl.ds(rows - width, width), :] += highs[s]
            first = pl.ds(0, length, stride=cycle)
            last = pl.ds(cycle - 1, length, stride=cycle)
            musc[nxt, s, first, :] = musc[nxt, s, first, :] + lefts[s]
            musc[nxt, s, last, :] = musc[nxt, s, last, :] + rights[s]

        every.wait_send()
        to_left.wait_send()
        to_right.wait_send()

        @pl.when(ax > 0)
        def _():
            low.wait_send()

        @pl.when(ax < n_ax - 1)
        def _():
            high.wait_send()

        return carry

    lax.fori_loop(0, TIME_STEPS, step, 0)
    final = TIME_STEPS % 2
    store_e = pltpu.make_async_copy(endo.at[final], endo_out, in_sems.at[0])
    store_m = pltpu.make_async_copy(musc.at[final], musc_out, in_sems.at[1])
    store_e.start()
    store_m.start()
    store_e.wait()
    store_m.wait()


def local(
    n_ax, n_circ,
    endothelium, muscle, agonist, proj_cell, proj_target, proj_count, endo_inverse, muscle_inverse
):
    n = n_ax * n_circ
    species, endo_ax, width, points = endothelium.shape
    length, cycle = muscle.shape[1:3]
    rows = endo_ax * width
    musc_rows = length * cycle
    slots = proj_cell.shape[2]
    live = jnp.arange(slots, dtype=jnp.int32)[None, :] < proj_count[0][:, None]
    marked = jnp.where(live, proj_target[0], musc_rows)
    arrived = lax.all_to_all(marked, ("ax", "circ"), split_axis=0, concat_axis=0, tiled=True)
    endo_ids = jnp.where(live, proj_cell[0], rows).T.reshape(-1)
    musc_ids = arrived.T.reshape(-1)
    vmem = pl.BlockSpec(memory_space=pltpu.VMEM)
    anywhere = pl.BlockSpec(memory_space=pl.ANY)
    dma = pltpu.SemaphoreType.DMA
    body = functools.partial(kernel, (n_ax, n_circ, width, length, cycle))
    endo_next, musc_next = pl.pallas_call(
        body,
        out_shape=(
            jax.ShapeDtypeStruct((species, rows, points), F32),
            jax.ShapeDtypeStruct((species, musc_rows, points), F32),
        ),
        in_specs=[anywhere, anywhere] + [vmem] * 7,
        out_specs=(anywhere, anywhere),
        scratch_shapes=[
            pltpu.VMEM((2, species, rows, points), F32),
            pltpu.VMEM((2, species, musc_rows, points), F32),
            pltpu.VMEM((2, species, width, points), F32),
            pltpu.VMEM((2, species, width, points), F32),
            pltpu.VMEM((2, species * length, points), F32),
            pltpu.VMEM((2, species * length, points), F32),
            pltpu.VMEM((2, species * length, points), F32),
            pltpu.VMEM((n, 16, points), F32),
            pltpu.VMEM((2, n, 16, points), F32),
            pltpu.VMEM((6, slots * n, points), F32),
            pltpu.VMEM((6, 2 * points, 2 * points), BF16),
            pltpu.VMEM((slots * n, rows), BF16),
            pltpu.VMEM((slots * n, musc_rows), BF16),
            pltpu.VMEM((rows, 2 * slots * n), BF16),
            pltpu.VMEM((musc_rows, 2 * slots * n), BF16),
            pltpu.VMEM((6, max(rows, musc_rows), 2 * points), BF16),
            dma((2,)), dma, dma, dma((2,)),
            dma((2,)), dma((2, 2)), dma((2,)), dma((2, 2)),
        ],
        compiler_params=pltpu.CompilerParams(
            collective_id=0, has_side_effects=True, vmem_limit_bytes=48 * 1024 * 1024
        ),
        name="cable_steps",
    )(
        endothelium.reshape(species, rows, points),
        muscle.reshape(species, musc_rows, points),
        agonist.reshape(rows, points),
        endo_ids[:, None], jnp.tile(endo_ids, 2)[None, :],
        musc_ids[:, None], jnp.tile(musc_ids, 2)[None, :],
        endo_inverse, muscle_inverse,
    )
    return endo_next.reshape(endothelium.shape), musc_next.reshape(muscle.shape)


def solution(mesh):
    tiles = P(None, "ax", "circ", None)
    sent = P(("ax", "circ"), None, None)
    return jax.shard_map(
        functools.partial(local, mesh.shape["ax"], mesh.shape["circ"]),
        mesh=mesh,
        in_specs=(tiles, tiles, P("ax", "circ", None), sent, sent, P(("ax", "circ"), None), P(), P()),
        out_specs=(tiles, tiles),
        check_vma=False,
    )
```

```python
import functools

import jax
import jax.numpy as jnp
from jax import lax
from jax.experimental import pallas as pl
from jax.experimental.pallas import tpu as pltpu
from jax.sharding import PartitionSpec as P

MESH = pl.DeviceIdType.MESH
TIME_STEPS = 8
DT = 0.2
COUPLING = (0.1, 0.3, 0.5)
ENDO_GAP = (0.05, 0.3, 0.5)
MUSC_GAP = (0.05, 0.1, 0.4)
BF16 = jnp.bfloat16
F32 = jnp.float32


def halves(x):
    high = x.astype(BF16)
    return high, (x - high.astype(F32)).astype(BF16)


def side_by_side(x):
    return jnp.concatenate(halves(x), axis=1)


def folded(y):
    half = y.shape[1] // 2
    return y[:, :half] + y[:, half:]


def dot(a, b):
    return jnp.dot(a, b, preferred_element_type=F32)


def reaction(u0, u1, u2, drive):
    square = u1 * u1
    release = square / (0.5 + square)
    second = -0.5 * u1 if drive is None else drive - 0.5 * u1
    return (1.2 * release - 0.6 * u0 - 0.2 * u2, second, 0.5 * u0 - 0.8 * u2)


def kernel(
    sizes,
    endo_in, musc_in, agonist_in, meta_in, endo_inv_in, musc_inv_in,
    endo_out, musc_out,
    endo, musc, halo_low, halo_high, edge_out, edge_left, edge_right,
    send, recv, picked, base_rows, weights, take_e, take_m, put_e, put_m, mix_e, mix_m, rhs,
    block_e, block_m, agonist, meta, meta_recv, endo_inv, musc_inv,
    in_sems, own_sem, send_sem, recv_sem, halo_send, halo_recv, edge_send, edge_recv,
    meta_sems,
):
    n_ax, n_circ, width, length, cycle = sizes
    n = n_ax * n_circ
    points = endo.shape[3]
    rows = endo.shape[2]
    musc_rows = musc.shape[2]
    ax = lax.axis_index("ax")
    circ = lax.axis_index("circ")
    me = ax * n_circ + circ
    right = lax.rem(circ + 1, n_circ)
    left = lax.rem(circ + n_circ - 1, n_circ)
    turned = [lax.rem(circ + c, n_circ) for c in range(n_circ)]

    def each_peer(act):
        def some(j, carry):
            far = lax.rem(ax + j, n_ax)
            for c in reversed(range(n_circ)):
                act(far, turned[c])
            return carry

        lax.fori_loop(1, n_ax, some, 0)
        for c in reversed(range(1, n_circ)):
            act(ax, turned[c])

    loads = [
        pltpu.make_async_copy(a, b, in_sems.at[i])
        for i, (a, b) in enumerate(
            (
                (meta_in, meta), (endo_in, endo.at[0]), (musc_in, musc.at[0]),
                (endo_inv_in, endo_inv), (musc_inv_in, musc_inv), (agonist_in, agonist),
            )
        )
    ]
    for load in loads:
        load.start()

    barrier = pltpu.get_barrier_semaphore()

    def greet(pa, pc):
        pl.semaphore_signal(barrier, inc=1, device_id=(pa, pc), device_id_type=MESH)

    each_peer(greet)

    @pl.when(ax == 0)
    def _():
        halo_low[...] = jnp.zeros_like(halo_low)

    @pl.when(ax == n_ax - 1)
    def _():
        halo_high[...] = jnp.zeros_like(halo_high)

    for load in loads:
        load.wait()
    pl.semaphore_wait(barrier, n - 1)

    def tell(pa, pc):
        pltpu.make_async_remote_copy(
            src_ref=meta.at[pa * n_circ + pc], dst_ref=meta_recv.at[me],
            send_sem=meta_sems.at[0], recv_sem=meta_sems.at[1],
            device_id=(pa, pc), device_id_type=MESH,
        ).start()

    each_peer(tell)
    own_meta = pltpu.make_async_copy(meta.at[me], meta_recv.at[me], own_sem)
    own_meta.start()

    for layer, inv in ((0, endo_inv), (1, musc_inv)):
        for s in range(3):
            row = side_by_side(inv[s].T)
            weights[layer * 3 + s] = jnp.concatenate([row, row], axis=0)

    def choose(ids, take, put):
        cells = lax.broadcasted_iota(jnp.int32, take.shape, 1)
        chosen = jnp.where(cells == ids, 1.0, 0.0)
        take[...] = chosen.astype(BF16)
        spread = chosen.T
        put[...] = jnp.concatenate([spread, spread], axis=1).astype(BF16)
        return chosen, dot(chosen.astype(BF16), spread.astype(BF16))

    sent = meta[:, 0, :]
    ids = jnp.concatenate([sent[:, 2:3], sent[:, 3:4]], axis=0)
    chosen, same = choose(ids, take_e, put_e)
    mix_e[...] = jnp.concatenate(
        [chosen[:, :width], chosen[:, rows - width:], same], axis=1
    ).astype(BF16)

    def gather(layer, s, values, out):
        take = take_e if layer == 0 else take_m
        out[layer * 3 + s] = folded(dot(take[...], side_by_side(values)))

    for s in range(3):
        gather(0, s, endo[0, s], picked)

    told = pltpu.make_async_remote_copy(
        src_ref=meta.at[pl.ds(0, n - 1)], dst_ref=meta_recv.at[pl.ds(0, n - 1)],
        send_sem=meta_sems.at[0], recv_sem=meta_sems.at[1],
        device_id=(ax, right), device_id_type=MESH,
    )
    told.wait_recv()
    own_meta.wait()
    got = meta_recv[:, 0, :]
    ids = jnp.concatenate([got[:, 0:1], got[:, 1:2]], axis=0)
    chosen, same = choose(ids, take_m, put_m)
    starts = lax.broadcasted_iota(jnp.int32, (ids.shape[0], length), 1) * cycle
    mix_m[...] = jnp.concatenate(
        [
            jnp.where(starts == ids, 1.0, 0.0),
            jnp.where(starts + (cycle - 1) == ids, 1.0, 0.0),
            same,
        ],
        axis=1,
    ).astype(BF16)
    for s in range(3):
        gather(1, s, musc[0, s], picked)
    told.wait_send()

    def messages(par):
        return pltpu.make_async_remote_copy(
            src_ref=send.at[par, pl.ds(0, n - 1), pl.ds(0, 12)],
            dst_ref=recv.at[par, pl.ds(0, n - 1), pl.ds(0, 12)],
            send_sem=send_sem.at[par], recv_sem=recv_sem.at[par],
            device_id=(ax, right), device_id_type=MESH,
        )

    def own_copy(par):
        return pltpu.make_async_copy(
            send.at[par, me, pl.ds(0, 12)], recv.at[par, me, pl.ds(0, 12)], own_sem
        )

    def pack(par):
        flat = send.at[par].reshape(n * 16, points)
        for q in range(6):
            for slot in range(2):
                flat[pl.ds(q * 2 + slot, n, stride=16), :] = picked[q, pl.ds(slot * n, n), :]

    def launch(par):
        def post(pa, pc):
            pltpu.make_async_remote_copy(
                src_ref=send.at[par, pa * n_circ + pc, pl.ds(0, 12)],
                dst_ref=recv.at[par, me, pl.ds(0, 12)],
                send_sem=send_sem.at[par],
                recv_sem=recv_sem.at[par],
                device_id=(pa, pc),
                device_id_type=MESH,
            ).start()

        each_peer(post)
        own_copy(par).start()

    def ends(par):
        low = pltpu.make_async_remote_copy(
            src_ref=endo.at[par, :, pl.ds(0, width)], dst_ref=halo_high.at[par],
            send_sem=halo_send.at[0], recv_sem=halo_recv.at[par, 0],
            device_id=(ax - 1, circ), device_id_type=MESH,
        )
        high = pltpu.make_async_remote_copy(
            src_ref=endo.at[par, :, pl.ds(rows - width, width)], dst_ref=halo_low.at[par],
            send_sem=halo_send.at[1], recv_sem=halo_recv.at[par, 1],
            device_id=(ax + 1, circ), device_id_type=MESH,
        )
        return low, high

    def sides(par):
        to_left = pltpu.make_async_remote_copy(
            src_ref=edge_out.at[0], dst_ref=edge_right.at[par],
            send_sem=edge_send.at[0], recv_sem=edge_recv.at[par, 0],
            device_id=(ax, left), device_id_type=MESH,
        )
        to_right = pltpu.make_async_remote_copy(
            src_ref=edge_out.at[1], dst_ref=edge_left.at[par],
            send_sem=edge_send.at[1], recv_sem=edge_recv.at[par, 1],
            device_id=(ax, right), device_id_type=MESH,
        )
        return to_left, to_right

    def start_ends(par):
        low, high = ends(par)
        pl.when(ax > 0)(low.start)
        pl.when(ax < n_ax - 1)(high.start)

    def start_sides(par):
        for s in range(3):
            span = pl.ds(s * length, length)
            edge_out[0, span] = musc[par, s, pl.ds(0, length, stride=cycle), :]
            edge_out[1, span] = musc[par, s, pl.ds(cycle - 1, length, stride=cycle), :]
        for copy in sides(par):
            copy.start()

    def local_part(par, nxt, last):
        count = rows // width
        for a in range(count):
            for j in range(0, width, 64):
                here = pl.ds(a * width + j, 64)
                u = [endo[par, s, here, :] for s in range(3)]
                parts = reaction(u[0], u[1], u[2], agonist[here, :])
                for s in range(3):
                    lap = -2.0 * u[s]
                    if a > 0:
                        lap = lap + endo[par, s, pl.ds((a - 1) * width + j, 64), :]
                    if a < count - 1:
                        lap = lap + endo[par, s, pl.ds((a + 1) * width + j, 64), :]
                    value = u[s] + DT * (parts[s] + ENDO_GAP[s] * lap)
                    rhs[s, here, :] = side_by_side(value)

        def musc_base(a, carry):
            here = pl.ds(pl.multiple_of(a * cycle, cycle), cycle)
            place_in = lax.broadcasted_iota(jnp.int32, (cycle, points), 0)
            u = [musc[par, s, here, :] for s in range(3)]
            parts = reaction(u[0], u[1], u[2], None)
            for s in range(3):
                before = jnp.where(place_in == 0, 0.0, pltpu.roll(u[s], 1, 0))
                after = jnp.where(place_in == cycle - 1, 0.0, pltpu.roll(u[s], cycle - 1, 0))
                lap = before + after - 2.0 * u[s]
                value = u[s] + DT * (parts[s] + MUSC_GAP[s] * lap)
                rhs[3 + s, here, :] = side_by_side(value)
            return carry

        lax.fori_loop(0, length, musc_base, 0)

        for layer, state in ((0, endo), (1, musc)):
            for s in range(3):
                value = folded(dot(rhs[layer * 3 + s], weights[layer * 3 + s]))
                state[nxt, s] = value
                if not last:
                    gather(layer, s, value, base_rows)

    def collect(par):
        own_copy(par).wait()
        messages(par).wait_recv()
        for copy in sides(par):
            copy.wait()
        low, high = ends(par)

        @pl.when(ax > 0)
        def _():
            low.wait_send()
            high.wait_recv()

        @pl.when(ax < n_ax - 1)
        def _():
            high.wait_send()
            low.wait_recv()

    def arrived(par, layer, s):
        flat = recv.at[par].reshape(n * 16, points)
        k = layer * 6 + s * 2
        return jnp.concatenate(
            [flat[pl.ds(k + slot, n, stride=16), :] for slot in range(2)], axis=0
        )

    def from_outside(par, last):
        for s in range(3):
            flux = (DT * COUPLING[s]) * (arrived(par, 1, s) - picked[s])
            gap = DT * ENDO_GAP[s]
            value = jnp.concatenate([gap * halo_low[par, s], gap * halo_high[par, s], flux], axis=0)
            value = folded(dot(side_by_side(value), weights[s]))
            block_e[s] = value
            fresh_e = None if last else base_rows[s] + folded(dot(mix_e[...], side_by_side(value)))
            flux = (DT * COUPLING[s]) * (arrived(par, 0, s) - picked[3 + s])
            gap = DT * MUSC_GAP[s]
            span = pl.ds(s * length, length)
            value = jnp.concatenate(
                [gap * edge_left[par, span, :], gap * edge_right[par, span, :], flux], axis=0
            )
            value = folded(dot(side_by_side(value), weights[3 + s]))
            block_m[s] = value
            if not last:
                picked[s] = fresh_e
                picked[3 + s] = base_rows[3 + s] + folded(dot(mix_m[...], side_by_side(value)))

    def finish_endo(nxt):
        flux = jnp.concatenate([block_e[s, pl.ds(2 * width, 2 * n), :] for s in range(3)], axis=1)
        gain = dot(put_e[...], jnp.concatenate(halves(flux), axis=0))
        for s in range(3):
            endo[nxt, s] += gain[:, s * points:(s + 1) * points]
            endo[nxt, s, pl.ds(0, width), :] += block_e[s, pl.ds(0, width), :]
            endo[nxt, s, pl.ds(rows - width, width), :] += block_e[s, pl.ds(width, width), :]

    def finish_musc(nxt):
        flux = jnp.concatenate([block_m[s, pl.ds(2 * length, 2 * n), :] for s in range(3)], axis=1)
        gain = dot(put_m[...], jnp.concatenate(halves(flux), axis=0))
        first = pl.ds(0, length, stride=cycle)
        final = pl.ds(cycle - 1, length, stride=cycle)
        for s in range(3):
            musc[nxt, s] += gain[:, s * points:(s + 1) * points]
            musc[nxt, s, first, :] = musc[nxt, s, first, :] + block_m[s, pl.ds(0, length), :]
            musc[nxt, s, final, :] = musc[nxt, s, final, :] + block_m[s, pl.ds(length, length), :]

    pack(0)
    launch(0)
    start_ends(0)
    start_sides(0)

    def step(t, carry):
        par = lax.rem(t, 2)
        nxt = 1 - par
        local_part(par, nxt, False)
        collect(par)
        from_outside(par, False)
        pl.when(t > 0)(lambda: messages(nxt).wait_send())
        pack(nxt)
        launch(nxt)
        finish_endo(nxt)
        start_ends(nxt)
        finish_musc(nxt)
        start_sides(nxt)
        return carry

    lax.fori_loop(0, TIME_STEPS - 1, step, 0)
    par = (TIME_STEPS - 1) % 2
    nxt = 1 - par
    local_part(par, nxt, True)
    collect(par)
    from_outside(par, True)
    finish_endo(nxt)
    store_e = pltpu.make_async_copy(endo.at[nxt], endo_out, in_sems.at[0])
    store_e.start()
    finish_musc(nxt)
    store_m = pltpu.make_async_copy(musc.at[nxt], musc_out, in_sems.at[1])
    store_m.start()
    messages(nxt).wait_send()
    messages(par).wait_send()
    store_e.wait()
    store_m.wait()


def local(
    n_ax, n_circ,
    endothelium, muscle, agonist, proj_cell, proj_target, proj_count, endo_inverse, muscle_inverse
):
    n = n_ax * n_circ
    species, endo_ax, width, points = endothelium.shape
    length, cycle = muscle.shape[1:3]
    rows = endo_ax * width
    musc_rows = length * cycle
    slots = proj_cell.shape[2]
    lane = jnp.arange(points, dtype=jnp.int32)[None, :]
    target, cell = proj_target[0], proj_cell[0]
    live = lane % slots < proj_count[0][:, None]
    first = jnp.where(lane == 0, target[:, 0:1], target[:, 1:2])
    second = jnp.where(lane == slots, cell[:, 0:1], cell[:, 1:2])
    meta = jnp.where(live, jnp.where(lane < slots, first, second), rows + musc_rows)
    anywhere = pl.BlockSpec(memory_space=pl.ANY)
    dma = pltpu.SemaphoreType.DMA
    body = functools.partial(kernel, (n_ax, n_circ, width, length, cycle))
    endo_next, musc_next = pl.pallas_call(
        body,
        out_shape=(
            jax.ShapeDtypeStruct((species, rows, points), F32),
            jax.ShapeDtypeStruct((species, musc_rows, points), F32),
        ),
        in_specs=[anywhere] * 6,
        out_specs=(anywhere, anywhere),
        scratch_shapes=[
            pltpu.VMEM((2, species, rows, points), F32),
            pltpu.VMEM((2, species, musc_rows, points), F32),
            pltpu.VMEM((2, species, width, points), F32),
            pltpu.VMEM((2, species, width, points), F32),
            pltpu.VMEM((2, species * length, points), F32),
            pltpu.VMEM((2, species * length, points), F32),
            pltpu.VMEM((2, species * length, points), F32),
            pltpu.VMEM((2, n, 16, points), F32),
            pltpu.VMEM((2, n, 16, points), F32),
            pltpu.VMEM((6, slots * n, points), F32),
            pltpu.VMEM((6, slots * n, points), F32),
            pltpu.VMEM((6, 2 * points, 2 * points), BF16),
            pltpu.VMEM((slots * n, rows), BF16),
            pltpu.VMEM((slots * n, musc_rows), BF16),
            pltpu.VMEM((rows, 2 * slots * n), BF16),
            pltpu.VMEM((musc_rows, 2 * slots * n), BF16),
            pltpu.VMEM((slots * n, 2 * width + slots * n), BF16),
            pltpu.VMEM((slots * n, 2 * length + slots * n), BF16),
            pltpu.VMEM((6, max(rows, musc_rows), 2 * points), BF16),
            pltpu.VMEM((species, 2 * width + slots * n, points), F32),
            pltpu.VMEM((species, 2 * length + slots * n, points), F32),
            pltpu.VMEM((rows, points), F32),
            pltpu.VMEM((n, 1, points), jnp.int32),
            pltpu.VMEM((n, 1, points), jnp.int32),
            pltpu.VMEM((species, points, points), F32),
            pltpu.VMEM((species, points, points), F32),
            dma((6,)), dma, dma((2,)), dma((2,)),
            dma((2,)), dma((2, 2)), dma((2,)), dma((2, 2)),
            dma((2,)),
        ],
        compiler_params=pltpu.CompilerParams(
            collective_id=0, has_side_effects=True, vmem_limit_bytes=60 * 1024 * 1024
        ),
        name="cable_steps",
    )(
        endothelium.reshape(species, rows, points),
        muscle.reshape(species, musc_rows, points),
        agonist.reshape(rows, points),
        meta[:, None, :],
        endo_inverse, muscle_inverse,
    )
    return endo_next.reshape(endothelium.shape), musc_next.reshape(muscle.shape)


def solution(mesh):
    tiles = P(None, "ax", "circ", None)
    sent = P(("ax", "circ"), None, None)
    return jax.shard_map(
        functools.partial(local, mesh.shape["ax"], mesh.shape["circ"]),
        mesh=mesh,
        in_specs=(tiles, tiles, P("ax", "circ", None), sent, sent, P(("ax", "circ"), None), P(), P()),
        out_specs=(tiles, tiles),
        check_vma=False,
    )
```

```python
import functools

import jax
import jax.numpy as jnp
from jax import lax
from jax.experimental import pallas as pl
from jax.experimental.pallas import tpu as pltpu
from jax.sharding import PartitionSpec as P

MESH = pl.DeviceIdType.MESH
TIME_STEPS = 8
DT = 0.2
COUPLING = (0.1, 0.3, 0.5)
ENDO_GAP = (0.05, 0.3, 0.5)
MUSC_GAP = (0.05, 0.1, 0.4)
BF16 = jnp.bfloat16
F32 = jnp.float32


def halves(x):
    high = x.astype(BF16)
    return high, (x - high.astype(F32)).astype(BF16)


def side_by_side(x):
    return jnp.concatenate(halves(x), axis=1)


def folded(y):
    half = y.shape[1] // 2
    return y[:, :half] + y[:, half:]


def dot(a, b):
    return jnp.dot(a, b, preferred_element_type=F32)


def reaction(u0, u1, u2, drive):
    square = u1 * u1
    release = square / (0.5 + square)
    second = -0.5 * u1 if drive is None else drive - 0.5 * u1
    return (1.2 * release - 0.6 * u0 - 0.2 * u2, second, 0.5 * u0 - 0.8 * u2)


def kernel(
    sizes,
    endo_in, musc_in, agonist_in, meta_in, endo_inv_in, musc_inv_in,
    endo_out, musc_out,
    endo, musc, halo_low, halo_high, edge_out, edge_left, edge_right,
    send, recv, picked, base_rows, weights, take_e, take_m, put_e, put_m, mix_e, mix_m, rhs,
    block_e, block_m, agonist, meta, meta_recv, endo_inv, musc_inv,
    in_sems, own_sem, send_sem, recv_sem, halo_send, halo_recv, edge_send, edge_recv,
    meta_sems, relay, relay_recv, relay_send,
):
    n_ax, n_circ, width, length, cycle = sizes
    n = n_ax * n_circ
    points = endo.shape[3]
    rows = endo.shape[2]
    musc_rows = musc.shape[2]
    ax = lax.axis_index("ax")
    circ = lax.axis_index("circ")
    me = ax * n_circ + circ
    right = lax.rem(circ + 1, n_circ)
    left = lax.rem(circ + n_circ - 1, n_circ)
    half = width // 2
    corners = n_ax % 4 == 0 and n_ax > 4
    turn = lax.rem(ax, 4)
    up_far = (turn == 3) & (ax < n_ax - 1)
    down_far = (turn == 0) & (ax > 0)
    relay_up = (turn == 3) & (ax > 3)
    relay_down = (turn == 0) & (ax < n_ax - 4)
    turned = [lax.rem(circ + c, n_circ) for c in range(n_circ)]

    def each_peer(act):
        def some(j, carry):
            far = lax.rem(ax + j, n_ax)
            for c in reversed(range(n_circ)):
                act(far, turned[c])
            return carry

        lax.fori_loop(1, n_ax, some, 0)
        for c in reversed(range(1, n_circ)):
            act(ax, turned[c])

    loads = [
        pltpu.make_async_copy(a, b, in_sems.at[i])
        for i, (a, b) in enumerate(
            (
                (meta_in, meta), (endo_in, endo.at[0]), (musc_in, musc.at[0]),
                (endo_inv_in, endo_inv), (musc_inv_in, musc_inv), (agonist_in, agonist),
            )
        )
    ]
    for load in loads:
        load.start()

    barrier = pltpu.get_barrier_semaphore()

    def greet(pa, pc):
        pl.semaphore_signal(barrier, inc=1, device_id=(pa, pc), device_id_type=MESH)

    each_peer(greet)

    @pl.when(ax == 0)
    def _():
        halo_low[...] = jnp.zeros_like(halo_low)

    @pl.when(ax == n_ax - 1)
    def _():
        halo_high[...] = jnp.zeros_like(halo_high)

    loads[0].wait()
    pl.semaphore_wait(barrier, n - 1)

    def tell(pa, pc):
        pltpu.make_async_remote_copy(
            src_ref=meta.at[pa * n_circ + pc], dst_ref=meta_recv.at[me],
            send_sem=meta_sems.at[0], recv_sem=meta_sems.at[1],
            device_id=(pa, pc), device_id_type=MESH,
        ).start()

    each_peer(tell)
    own_meta = pltpu.make_async_copy(meta.at[me], meta_recv.at[me], own_sem)
    own_meta.start()

    loads[3].wait()
    loads[4].wait()
    for layer, inv in ((0, endo_inv), (1, musc_inv)):
        for s in range(3):
            row = side_by_side(inv[s].T)
            weights[layer * 3 + s] = jnp.concatenate([row, row], axis=0)

    def choose(ids, take, put):
        cells = lax.broadcasted_iota(jnp.int32, take.shape, 1)
        chosen = jnp.where(cells == ids, 1.0, 0.0)
        take[...] = chosen.astype(BF16)
        spread = chosen.T
        put[...] = jnp.concatenate([spread, spread], axis=1).astype(BF16)
        return chosen, dot(chosen.astype(BF16), spread.astype(BF16))

    sent = meta[:, 0, :]
    ids = jnp.concatenate([sent[:, 2:3], sent[:, 3:4]], axis=0)
    chosen, same = choose(ids, take_e, put_e)
    mix_e[...] = jnp.concatenate(
        [chosen[:, :width], chosen[:, rows - width:], same], axis=1
    ).astype(BF16)

    def gather(layer, s, values, out):
        take = take_e if layer == 0 else take_m
        out[layer * 3 + s] = folded(dot(take[...], side_by_side(values)))

    loads[1].wait()
    loads[2].wait()
    loads[5].wait()
    for s in range(3):
        gather(0, s, endo[0, s], picked)

    told = pltpu.make_async_remote_copy(
        src_ref=meta.at[pl.ds(0, n - 1)], dst_ref=meta_recv.at[pl.ds(0, n - 1)],
        send_sem=meta_sems.at[0], recv_sem=meta_sems.at[1],
        device_id=(ax, right), device_id_type=MESH,
    )
    told.wait_recv()
    own_meta.wait()
    got = meta_recv[:, 0, :]
    ids = jnp.concatenate([got[:, 0:1], got[:, 1:2]], axis=0)
    chosen, same = choose(ids, take_m, put_m)
    starts = lax.broadcasted_iota(jnp.int32, (ids.shape[0], length), 1) * cycle
    mix_m[...] = jnp.concatenate(
        [
            jnp.where(starts == ids, 1.0, 0.0),
            jnp.where(starts + (cycle - 1) == ids, 1.0, 0.0),
            same,
        ],
        axis=1,
    ).astype(BF16)
    for s in range(3):
        gather(1, s, musc[0, s], picked)
    told.wait_send()

    def messages(par):
        return pltpu.make_async_remote_copy(
            src_ref=send.at[par, pl.ds(0, n - 1), pl.ds(0, 12)],
            dst_ref=recv.at[par, pl.ds(0, n - 1), pl.ds(0, 12)],
            send_sem=send_sem.at[par], recv_sem=recv_sem.at[par],
            device_id=(ax, right), device_id_type=MESH,
        )

    def own_copy(par):
        return pltpu.make_async_copy(
            send.at[par, me, pl.ds(0, 12)], recv.at[par, me, pl.ds(0, 12)], own_sem
        )

    def pack(par):
        flat = send.at[par].reshape(n * 16, points)
        for q in range(6):
            for slot in range(2):
                flat[pl.ds(q * 2 + slot, n, stride=16), :] = picked[q, pl.ds(slot * n, n), :]

    def launch(par):
        def post(pa, pc):
            pltpu.make_async_remote_copy(
                src_ref=send.at[par, pa * n_circ + pc, pl.ds(0, 12)],
                dst_ref=recv.at[par, me, pl.ds(0, 12)],
                send_sem=send_sem.at[par],
                recv_sem=recv_sem.at[par],
                device_id=(pa, pc),
                device_id_type=MESH,
            ).start()

        each_peer(post)
        own_copy(par).start()

    def cells(par, from_top, start, count):
        first = rows - width if from_top else 0
        return endo.at[par, :, pl.ds(first + start, count)]

    def end_copy(par, up, start, count):
        dst = halo_low if up else halo_high
        return pltpu.make_async_remote_copy(
            src_ref=cells(par, up, start, count), dst_ref=dst.at[par, :, pl.ds(start, count)],
            send_sem=halo_send.at[int(up)], recv_sem=halo_recv.at[par, int(up)],
            device_id=(ax + 1 if up else ax - 1, circ), device_id_type=MESH,
        )

    def to_relay(par, up):
        return pltpu.make_async_remote_copy(
            src_ref=cells(par, up, half, width - half), dst_ref=relay.at[par, int(up)],
            send_sem=halo_send.at[int(up)], recv_sem=relay_recv.at[par, int(up)],
            device_id=(ax + 4 if up else ax - 4, circ), device_id_type=MESH,
        )

    def from_relay(par, up):
        dst = halo_low if up else halo_high
        return pltpu.make_async_remote_copy(
            src_ref=relay.at[par, int(up)], dst_ref=dst.at[par, :, pl.ds(half, width - half)],
            send_sem=relay_send.at[int(up)], recv_sem=halo_recv.at[par, int(up)],
            device_id=(ax - 3 if up else ax + 3, circ), device_id_type=MESH,
        )

    def start_far(par):
        if corners:
            pl.when(up_far)(to_relay(par, True).start)
            pl.when(down_far)(to_relay(par, False).start)

    def start_ends(par):
        if corners:
            pl.when(up_far)(end_copy(par, True, 0, half).start)
            pl.when(down_far)(end_copy(par, False, 0, half).start)
            pl.when((ax < n_ax - 1) & (turn != 3))(end_copy(par, True, 0, width).start)
            pl.when((ax > 0) & (turn != 0))(end_copy(par, False, 0, width).start)
        else:
            pl.when(ax < n_ax - 1)(end_copy(par, True, 0, width).start)
            pl.when(ax > 0)(end_copy(par, False, 0, width).start)

    def pass_on(par):
        if not corners:
            return
        for up, here in ((True, relay_up), (False, relay_down)):

            @pl.when(here)
            def _():
                to_relay(par, up).wait_recv()
                from_relay(par, up).start()

    def passed_on(par):
        if corners:
            pl.when(relay_up)(from_relay(par, True).wait_send)
            pl.when(relay_down)(from_relay(par, False).wait_send)

    def sides(par):
        to_left = pltpu.make_async_remote_copy(
            src_ref=edge_out.at[0], dst_ref=edge_right.at[par],
            send_sem=edge_send.at[0], recv_sem=edge_recv.at[par, 0],
            device_id=(ax, left), device_id_type=MESH,
        )
        to_right = pltpu.make_async_remote_copy(
            src_ref=edge_out.at[1], dst_ref=edge_left.at[par],
            send_sem=edge_send.at[1], recv_sem=edge_recv.at[par, 1],
            device_id=(ax, right), device_id_type=MESH,
        )
        return to_left, to_right

    def start_sides(par):
        for s in range(3):
            span = pl.ds(s * length, length)
            edge_out[0, span] = musc[par, s, pl.ds(0, length, stride=cycle), :]
            edge_out[1, span] = musc[par, s, pl.ds(cycle - 1, length, stride=cycle), :]
        for copy in sides(par):
            copy.start()

    def local_part(par, nxt, last):
        count = rows // width
        for a in range(count):
            for j in range(0, width, 64):
                here = pl.ds(a * width + j, 64)
                u = [endo[par, s, here, :] for s in range(3)]
                parts = reaction(u[0], u[1], u[2], agonist[here, :])
                for s in range(3):
                    lap = -2.0 * u[s]
                    if a > 0:
                        lap = lap + endo[par, s, pl.ds((a - 1) * width + j, 64), :]
                    if a < count - 1:
                        lap = lap + endo[par, s, pl.ds((a + 1) * width + j, 64), :]
                    value = u[s] + DT * (parts[s] + ENDO_GAP[s] * lap)
                    rhs[s, here, :] = side_by_side(value)

        def musc_base(a, carry):
            here = pl.ds(pl.multiple_of(a * cycle, cycle), cycle)
            place_in = lax.broadcasted_iota(jnp.int32, (cycle, points), 0)
            u = [musc[par, s, here, :] for s in range(3)]
            parts = reaction(u[0], u[1], u[2], None)
            for s in range(3):
                before = jnp.where(place_in == 0, 0.0, pltpu.roll(u[s], 1, 0))
                after = jnp.where(place_in == cycle - 1, 0.0, pltpu.roll(u[s], cycle - 1, 0))
                lap = before + after - 2.0 * u[s]
                value = u[s] + DT * (parts[s] + MUSC_GAP[s] * lap)
                rhs[3 + s, here, :] = side_by_side(value)
            return carry

        lax.fori_loop(0, length, musc_base, 0)
        pass_on(par)

        for layer, state in ((0, endo), (1, musc)):
            for s in range(3):
                value = folded(dot(rhs[layer * 3 + s], weights[layer * 3 + s]))
                state[nxt, s] = value
                if not last:
                    gather(layer, s, value, base_rows)

    def collect(par):
        own_copy(par).wait()
        messages(par).wait_recv()
        for copy in sides(par):
            copy.wait()
        passed_on(par)

        @pl.when(ax > 0)
        def _():
            end_copy(par, False, 0, width).wait_send()
            end_copy(par, True, 0, width).wait_recv()

        @pl.when(ax < n_ax - 1)
        def _():
            end_copy(par, True, 0, width).wait_send()
            end_copy(par, False, 0, width).wait_recv()

    def arrived(par, layer, s):
        flat = recv.at[par].reshape(n * 16, points)
        k = layer * 6 + s * 2
        return jnp.concatenate(
            [flat[pl.ds(k + slot, n, stride=16), :] for slot in range(2)], axis=0
        )

    def endo_outside(par):
        for s in range(3):
            flux = (DT * COUPLING[s]) * (arrived(par, 1, s) - picked[s])
            gap = DT * ENDO_GAP[s]
            value = jnp.concatenate([gap * halo_low[par, s], gap * halo_high[par, s], flux], axis=0)
            block_e[s] = folded(dot(side_by_side(value), weights[s]))

    def musc_outside(par):
        for s in range(3):
            flux = (DT * COUPLING[s]) * (arrived(par, 0, s) - picked[3 + s])
            gap = DT * MUSC_GAP[s]
            span = pl.ds(s * length, length)
            value = jnp.concatenate(
                [gap * edge_left[par, span, :], gap * edge_right[par, span, :], flux], axis=0
            )
            block_m[s] = folded(dot(side_by_side(value), weights[3 + s]))

    def pick():
        for s in range(3):
            picked[s] = base_rows[s] + folded(dot(mix_e[...], side_by_side(block_e[s])))
            picked[3 + s] = base_rows[3 + s] + folded(dot(mix_m[...], side_by_side(block_m[s])))

    def endo_flux():
        flux = jnp.concatenate([block_e[s, pl.ds(2 * width, 2 * n), :] for s in range(3)], axis=1)
        return jnp.concatenate(halves(flux), axis=0)

    def finish_ends(nxt):
        flux = endo_flux()
        for i, first in enumerate((0, rows - width)):
            span = pl.ds(first, width)
            gain = dot(put_e[span, :], flux)
            for s in range(3):
                endo[nxt, s, span, :] += (
                    gain[:, s * points:(s + 1) * points] + block_e[s, pl.ds(i * width, width), :]
                )

    def finish_inside(nxt):
        span = pl.ds(width, rows - 2 * width)
        gain = dot(put_e[span, :], endo_flux())
        for s in range(3):
            endo[nxt, s, span, :] += gain[:, s * points:(s + 1) * points]

    def finish_musc(nxt):
        flux = jnp.concatenate([block_m[s, pl.ds(2 * length, 2 * n), :] for s in range(3)], axis=1)
        gain = dot(put_m[...], jnp.concatenate(halves(flux), axis=0))
        first = pl.ds(0, length, stride=cycle)
        final = pl.ds(cycle - 1, length, stride=cycle)
        for s in range(3):
            musc[nxt, s] += gain[:, s * points:(s + 1) * points]
            musc[nxt, s, first, :] = musc[nxt, s, first, :] + block_m[s, pl.ds(0, length), :]
            musc[nxt, s, final, :] = musc[nxt, s, final, :] + block_m[s, pl.ds(length, length), :]

    start_far(0)
    pack(0)
    launch(0)
    start_ends(0)
    start_sides(0)

    def step(t, carry):
        par = lax.rem(t, 2)
        nxt = 1 - par
        local_part(par, nxt, False)
        collect(par)
        endo_outside(par)
        finish_ends(nxt)
        start_far(nxt)
        musc_outside(par)
        pick()
        pl.when(t > 0)(lambda: messages(nxt).wait_send())
        pack(nxt)
        launch(nxt)
        start_ends(nxt)
        finish_musc(nxt)
        start_sides(nxt)
        finish_inside(nxt)
        return carry

    lax.fori_loop(0, TIME_STEPS - 1, step, 0)
    par = (TIME_STEPS - 1) % 2
    nxt = 1 - par
    local_part(par, nxt, True)
    collect(par)
    endo_outside(par)
    finish_ends(nxt)
    finish_inside(nxt)
    store_e = pltpu.make_async_copy(endo.at[nxt], endo_out, in_sems.at[0])
    store_e.start()
    musc_outside(par)
    finish_musc(nxt)
    store_m = pltpu.make_async_copy(musc.at[nxt], musc_out, in_sems.at[1])
    store_m.start()
    messages(nxt).wait_send()
    messages(par).wait_send()
    store_e.wait()
    store_m.wait()


def hand_over(endo_from, musc_from, endo_to, musc_to, sems):
    copies = []
    for layer, (a, b) in enumerate(((endo_from, endo_to), (musc_from, musc_to))):
        for s in range(a.shape[0]):
            copies.append(pltpu.make_async_copy(a.at[s], b.at[s], sems.at[layer, s]))
    for copy in copies:
        copy.start()
    for copy in copies:
        copy.wait()


def local(
    n_ax, n_circ,
    endothelium, muscle, agonist, proj_cell, proj_target, proj_count, endo_inverse, muscle_inverse
):
    n = n_ax * n_circ
    species, endo_ax, width, points = endothelium.shape
    length, cycle = muscle.shape[1:3]
    rows = endo_ax * width
    musc_rows = length * cycle
    slots = proj_cell.shape[2]
    lane = jnp.arange(points, dtype=jnp.int32)[None, :]
    target, cell = proj_target[0], proj_cell[0]
    live = lane % slots < proj_count[0][:, None]
    first = jnp.where(lane == 0, target[:, 0:1], target[:, 1:2])
    second = jnp.where(lane == slots, cell[:, 0:1], cell[:, 1:2])
    meta = jnp.where(live, jnp.where(lane < slots, first, second), rows + musc_rows)
    anywhere = pl.BlockSpec(memory_space=pl.ANY)
    dma = pltpu.SemaphoreType.DMA
    body = functools.partial(kernel, (n_ax, n_circ, width, length, cycle))
    endo_next, musc_next = pl.pallas_call(
        body,
        out_shape=(
            jax.ShapeDtypeStruct((species, rows, points), F32),
            jax.ShapeDtypeStruct((species, musc_rows, points), F32),
        ),
        in_specs=[anywhere] * 6,
        out_specs=(anywhere, anywhere),
        scratch_shapes=[
            pltpu.VMEM((2, species, rows, points), F32),
            pltpu.VMEM((2, species, musc_rows, points), F32),
            pltpu.VMEM((2, species, width, points), F32),
            pltpu.VMEM((2, species, width, points), F32),
            pltpu.VMEM((2, species * length, points), F32),
            pltpu.VMEM((2, species * length, points), F32),
            pltpu.VMEM((2, species * length, points), F32),
            pltpu.VMEM((2, n, 16, points), F32),
            pltpu.VMEM((2, n, 16, points), F32),
            pltpu.VMEM((6, slots * n, points), F32),
            pltpu.VMEM((6, slots * n, points), F32),
            pltpu.VMEM((6, 2 * points, 2 * points), BF16),
            pltpu.VMEM((slots * n, rows), BF16),
            pltpu.VMEM((slots * n, musc_rows), BF16),
            pltpu.VMEM((rows, 2 * slots * n), BF16),
            pltpu.VMEM((musc_rows, 2 * slots * n), BF16),
            pltpu.VMEM((slots * n, 2 * width + slots * n), BF16),
            pltpu.VMEM((slots * n, 2 * length + slots * n), BF16),
            pltpu.VMEM((6, max(rows, musc_rows), 2 * points), BF16),
            pltpu.VMEM((species, 2 * width + slots * n, points), F32),
            pltpu.VMEM((species, 2 * length + slots * n, points), F32),
            pltpu.VMEM((rows, points), F32),
            pltpu.VMEM((n, 1, points), jnp.int32),
            pltpu.VMEM((n, 1, points), jnp.int32),
            pltpu.VMEM((species, points, points), F32),
            pltpu.VMEM((species, points, points), F32),
            dma((6,)), dma, dma((2,)), dma((2,)),
            dma((2,)), dma((2, 2)), dma((2,)), dma((2, 2)),
            dma((2,)),
            pltpu.VMEM((2, 2, species, width - width // 2, points), F32),
            dma((2, 2)), dma((2,)),
        ],
        compiler_params=pltpu.CompilerParams(
            collective_id=0, has_side_effects=True, vmem_limit_bytes=60 * 1024 * 1024
        ),
        name="cable_steps",
    )(
        endothelium.reshape(species, rows, points),
        muscle.reshape(species, musc_rows, points),
        agonist.reshape(rows, points),
        meta[:, None, :],
        endo_inverse, muscle_inverse,
    )
    endo_next, musc_next = pl.pallas_call(
        hand_over,
        out_shape=(
            jax.ShapeDtypeStruct((species, rows, points), F32),
            jax.ShapeDtypeStruct((species, musc_rows, points), F32),
        ),
        in_specs=[anywhere] * 2,
        out_specs=(anywhere, anywhere),
        scratch_shapes=[dma((2, species))],
        compiler_params=pltpu.CompilerParams(vmem_limit_bytes=60 * 1024 * 1024),
        name="hand_over",
    )(endo_next, musc_next)
    return endo_next.reshape(endothelium.shape), musc_next.reshape(muscle.shape)


def solution(mesh):
    tiles = P(None, "ax", "circ", None)
    sent = P(("ax", "circ"), None, None)
    return jax.shard_map(
        functools.partial(local, mesh.shape["ax"], mesh.shape["circ"]),
        mesh=mesh,
        in_specs=(tiles, tiles, P("ax", "circ", None), sent, sent, P(("ax", "circ"), None), P(), P()),
        out_specs=(tiles, tiles),
        check_vma=False,
    )
```

```python
import functools

import jax
import jax.numpy as jnp
from jax import lax
from jax.experimental import pallas as pl
from jax.experimental.pallas import tpu as pltpu
from jax.sharding import PartitionSpec as P

MESH = pl.DeviceIdType.MESH
TIME_STEPS = 8
DT = 0.2
COUPLING = (0.1, 0.3, 0.5)
ENDO_GAP = (0.05, 0.3, 0.5)
MUSC_GAP = (0.05, 0.1, 0.4)
BF16 = jnp.bfloat16
F32 = jnp.float32


def halves(x):
    high = x.astype(BF16)
    return high, (x - high.astype(F32)).astype(BF16)


def side_by_side(x):
    return jnp.concatenate(halves(x), axis=1)


def folded(y):
    half = y.shape[1] // 2
    return y[:, :half] + y[:, half:]


def dot(a, b):
    return jnp.dot(a, b, preferred_element_type=F32)


def reaction(u0, u1, u2, drive):
    square = u1 * u1
    release = square / (0.5 + square)
    second = -0.5 * u1 if drive is None else drive - 0.5 * u1
    return (1.2 * release - 0.6 * u0 - 0.2 * u2, second, 0.5 * u0 - 0.8 * u2)


def kernel(
    sizes,
    endo_in, musc_in, agonist_in, meta_in, endo_inv_in, musc_inv_in,
    endo_out, musc_out,
    endo, musc, halo_low, halo_high, edge_out, edge_left, edge_right,
    send, recv, picked, base_rows, weights, take_e, take_m, put_e, put_m, mix_e, mix_m, same_e, same_m, rhs,
    block_e, block_m, agonist, meta, meta_recv, endo_inv, musc_inv,
    in_sems, own_sem, send_sem, recv_sem, halo_send, halo_recv, edge_send, edge_recv,
    meta_sems, relay, relay_recv, relay_send,
):
    n_ax, n_circ, width, length, cycle = sizes
    n = n_ax * n_circ
    points = endo.shape[3]
    rows = endo.shape[2]
    musc_rows = musc.shape[2]
    ax = lax.axis_index("ax")
    circ = lax.axis_index("circ")
    me = ax * n_circ + circ
    right = lax.rem(circ + 1, n_circ)
    left = lax.rem(circ + n_circ - 1, n_circ)
    half = width // 2
    corners = n_ax % 4 == 0 and n_ax > 4
    turn = lax.rem(ax, 4)
    up_far = (turn == 3) & (ax < n_ax - 1)
    down_far = (turn == 0) & (ax > 0)
    relay_up = (turn == 0) & (ax < n_ax - 4)
    relay_down = (turn == 3) & (ax > 3)
    turned = [lax.rem(circ + c, n_circ) for c in range(n_circ)]

    def each_peer(act):
        def some(j, carry):
            far = lax.rem(ax + j, n_ax)
            for c in reversed(range(n_circ)):
                act(far, turned[c])
            return carry

        lax.fori_loop(1, n_ax, some, 0)
        for c in reversed(range(1, n_circ)):
            act(ax, turned[c])

    loads = [
        pltpu.make_async_copy(a, b, in_sems.at[i])
        for i, (a, b) in enumerate(
            (
                (meta_in, meta), (endo_in, endo.at[0]), (musc_in, musc.at[0]),
                (endo_inv_in, endo_inv), (musc_inv_in, musc_inv), (agonist_in, agonist),
            )
        )
    ]
    for load in loads:
        load.start()

    barrier = pltpu.get_barrier_semaphore()

    def greet(pa, pc):
        pl.semaphore_signal(barrier, inc=1, device_id=(pa, pc), device_id_type=MESH)

    each_peer(greet)

    @pl.when(ax == 0)
    def _():
        halo_low[...] = jnp.zeros_like(halo_low)

    @pl.when(ax == n_ax - 1)
    def _():
        halo_high[...] = jnp.zeros_like(halo_high)

    loads[0].wait()
    pl.semaphore_wait(barrier, n - 1)

    def tell(pa, pc):
        pltpu.make_async_remote_copy(
            src_ref=meta.at[pa * n_circ + pc], dst_ref=meta_recv.at[me],
            send_sem=meta_sems.at[0], recv_sem=meta_sems.at[1],
            device_id=(pa, pc), device_id_type=MESH,
        ).start()

    each_peer(tell)
    own_meta = pltpu.make_async_copy(meta.at[me], meta_recv.at[me], own_sem)
    own_meta.start()

    loads[3].wait()
    loads[4].wait()
    for layer, inv in ((0, endo_inv), (1, musc_inv)):
        for s in range(3):
            row = side_by_side(inv[s].T)
            weights[layer * 3 + s] = jnp.concatenate([row, row], axis=0)

    def choose(ids, take, put):
        cells = lax.broadcasted_iota(jnp.int32, take.shape, 1)
        chosen = jnp.where(cells == ids, 1.0, 0.0)
        take[...] = chosen.astype(BF16)
        spread = chosen.T
        put[...] = jnp.concatenate([spread, spread], axis=1).astype(BF16)
        return chosen, dot(chosen.astype(BF16), spread.astype(BF16))

    sent = meta[:, 0, :]
    ids = jnp.concatenate([sent[:, 2:3], sent[:, 3:4]], axis=0)
    chosen, same = choose(ids, take_e, put_e)
    mix_e[...] = jnp.concatenate([chosen[:, :width], chosen[:, rows - width:]], axis=1).astype(BF16)
    same_e[...] = same.astype(BF16)

    def gather(layer, s, values, out):
        take = take_e if layer == 0 else take_m
        out[layer * 3 + s] = folded(dot(take[...], side_by_side(values)))

    loads[1].wait()
    loads[2].wait()
    loads[5].wait()
    for s in range(3):
        gather(0, s, endo[0, s], picked)

    told = pltpu.make_async_remote_copy(
        src_ref=meta.at[pl.ds(0, n - 1)], dst_ref=meta_recv.at[pl.ds(0, n - 1)],
        send_sem=meta_sems.at[0], recv_sem=meta_sems.at[1],
        device_id=(ax, right), device_id_type=MESH,
    )
    told.wait_recv()
    own_meta.wait()
    got = meta_recv[:, 0, :]
    ids = jnp.concatenate([got[:, 0:1], got[:, 1:2]], axis=0)
    chosen, same = choose(ids, take_m, put_m)
    starts = lax.broadcasted_iota(jnp.int32, (ids.shape[0], length), 1) * cycle
    mix_m[...] = jnp.concatenate(
        [
            jnp.where(starts == ids, 1.0, 0.0),
            jnp.where(starts + (cycle - 1) == ids, 1.0, 0.0),
        ],
        axis=1,
    ).astype(BF16)
    same_m[...] = same.astype(BF16)
    for s in range(3):
        gather(1, s, musc[0, s], picked)
    told.wait_send()

    def messages(par):
        return pltpu.make_async_remote_copy(
            src_ref=send.at[par, pl.ds(0, n - 1), pl.ds(0, 12)],
            dst_ref=recv.at[par, pl.ds(0, n - 1), pl.ds(0, 12)],
            send_sem=send_sem.at[par], recv_sem=recv_sem.at[par],
            device_id=(ax, right), device_id_type=MESH,
        )

    def own_copy(par):
        return pltpu.make_async_copy(
            send.at[par, me, pl.ds(0, 12)], recv.at[par, me, pl.ds(0, 12)], own_sem
        )

    def pack(par):
        flat = send.at[par].reshape(n * 16, points)
        for q in range(6):
            for slot in range(2):
                flat[pl.ds(q * 2 + slot, n, stride=16), :] = picked[q, pl.ds(slot * n, n), :]

    def launch(par):
        def post(pa, pc):
            pltpu.make_async_remote_copy(
                src_ref=send.at[par, pa * n_circ + pc, pl.ds(0, 12)],
                dst_ref=recv.at[par, me, pl.ds(0, 12)],
                send_sem=send_sem.at[par],
                recv_sem=recv_sem.at[par],
                device_id=(pa, pc),
                device_id_type=MESH,
            ).start()

        each_peer(post)
        own_copy(par).start()

    def cells(par, from_top, start, count):
        first = rows - width if from_top else 0
        return endo.at[par, :, pl.ds(first + start, count)]

    def end_copy(par, up, start, count):
        dst = halo_low if up else halo_high
        return pltpu.make_async_remote_copy(
            src_ref=cells(par, up, start, count), dst_ref=dst.at[par, :, pl.ds(start, count)],
            send_sem=halo_send.at[int(up)], recv_sem=halo_recv.at[par, int(up)],
            device_id=(ax + 1 if up else ax - 1, circ), device_id_type=MESH,
        )

    def to_relay(par, up):
        return pltpu.make_async_remote_copy(
            src_ref=cells(par, up, half, width - half), dst_ref=relay.at[par, int(up)],
            send_sem=halo_send.at[int(up)], recv_sem=relay_recv.at[par, int(up)],
            device_id=(ax - 3 if up else ax + 3, circ), device_id_type=MESH,
        )

    def from_relay(par, up):
        dst = halo_low if up else halo_high
        return pltpu.make_async_remote_copy(
            src_ref=relay.at[par, int(up)], dst_ref=dst.at[par, :, pl.ds(half, width - half)],
            send_sem=relay_send.at[int(up)], recv_sem=halo_recv.at[par, int(up)],
            device_id=(ax + 4 if up else ax - 4, circ), device_id_type=MESH,
        )

    def start_far(par):
        if corners:
            pl.when(up_far)(to_relay(par, True).start)
            pl.when(down_far)(to_relay(par, False).start)

    def start_ends(par):
        if corners:
            pl.when(up_far)(end_copy(par, True, 0, half).start)
            pl.when(down_far)(end_copy(par, False, 0, half).start)
            pl.when((ax < n_ax - 1) & (turn != 3))(end_copy(par, True, 0, width).start)
            pl.when((ax > 0) & (turn != 0))(end_copy(par, False, 0, width).start)
        else:
            pl.when(ax < n_ax - 1)(end_copy(par, True, 0, width).start)
            pl.when(ax > 0)(end_copy(par, False, 0, width).start)

    def pass_on(par):
        if not corners:
            return
        for up, here in ((True, relay_up), (False, relay_down)):

            @pl.when(here)
            def _():
                to_relay(par, up).wait_recv()
                from_relay(par, up).start()

    def passed_on(par):
        if corners:
            pl.when(relay_up)(from_relay(par, True).wait_send)
            pl.when(relay_down)(from_relay(par, False).wait_send)

    def sides(par):
        to_left = pltpu.make_async_remote_copy(
            src_ref=edge_out.at[0], dst_ref=edge_right.at[par],
            send_sem=edge_send.at[0], recv_sem=edge_recv.at[par, 0],
            device_id=(ax, left), device_id_type=MESH,
        )
        to_right = pltpu.make_async_remote_copy(
            src_ref=edge_out.at[1], dst_ref=edge_left.at[par],
            send_sem=edge_send.at[1], recv_sem=edge_recv.at[par, 1],
            device_id=(ax, right), device_id_type=MESH,
        )
        return to_left, to_right

    def start_sides(par):
        for s in range(3):
            span = pl.ds(s * length, length)
            edge_out[0, span] = musc[par, s, pl.ds(0, length, stride=cycle), :]
            edge_out[1, span] = musc[par, s, pl.ds(cycle - 1, length, stride=cycle), :]
        for copy in sides(par):
            copy.start()

    def local_part(par, nxt, last):
        count = rows // width
        for a in range(count):
            for j in range(0, width, 64):
                here = pl.ds(a * width + j, 64)
                u = [endo[par, s, here, :] for s in range(3)]
                parts = reaction(u[0], u[1], u[2], agonist[here, :])
                for s in range(3):
                    lap = -2.0 * u[s]
                    if a > 0:
                        lap = lap + endo[par, s, pl.ds((a - 1) * width + j, 64), :]
                    if a < count - 1:
                        lap = lap + endo[par, s, pl.ds((a + 1) * width + j, 64), :]
                    value = u[s] + DT * (parts[s] + ENDO_GAP[s] * lap)
                    rhs[s, here, :] = side_by_side(value)

        def musc_base(a, carry):
            here = pl.ds(pl.multiple_of(a * cycle, cycle), cycle)
            place_in = lax.broadcasted_iota(jnp.int32, (cycle, points), 0)
            u = [musc[par, s, here, :] for s in range(3)]
            parts = reaction(u[0], u[1], u[2], None)
            for s in range(3):
                before = jnp.where(place_in == 0, 0.0, pltpu.roll(u[s], 1, 0))
                after = jnp.where(place_in == cycle - 1, 0.0, pltpu.roll(u[s], cycle - 1, 0))
                lap = before + after - 2.0 * u[s]
                value = u[s] + DT * (parts[s] + MUSC_GAP[s] * lap)
                rhs[3 + s, here, :] = side_by_side(value)
            return carry

        lax.fori_loop(0, length, musc_base, 0)
        pass_on(par)

        for layer, state in ((0, endo), (1, musc)):
            for s in range(3):
                value = folded(dot(rhs[layer * 3 + s], weights[layer * 3 + s]))
                state[nxt, s] = value
                if not last:
                    gather(layer, s, value, base_rows)

    def collect_messages(par):
        own_copy(par).wait()
        messages(par).wait_recv()

    def collect_halos(par):
        for copy in sides(par):
            copy.wait()
        passed_on(par)

        @pl.when(ax > 0)
        def _():
            end_copy(par, False, 0, width).wait_send()
            end_copy(par, True, 0, width).wait_recv()

        @pl.when(ax < n_ax - 1)
        def _():
            end_copy(par, True, 0, width).wait_send()
            end_copy(par, False, 0, width).wait_recv()

    def arrived(par, layer, s):
        flat = recv.at[par].reshape(n * 16, points)
        k = layer * 6 + s * 2
        return jnp.concatenate(
            [flat[pl.ds(k + slot, n, stride=16), :] for slot in range(2)], axis=0
        )

    def inverted(layer, s, value):
        return folded(dot(side_by_side(value), weights[layer * 3 + s]))

    def take_messages(par, last=False):
        for s in range(3):
            flux = (DT * COUPLING[s]) * (arrived(par, 1, s) - picked[s])
            flux = inverted(0, s, flux)
            block_e[s, pl.ds(2 * width, 2 * n), :] = flux
            if not last:
                picked[s] = base_rows[s] + folded(dot(same_e[...], side_by_side(flux)))
            flux = (DT * COUPLING[s]) * (arrived(par, 0, s) - picked[3 + s])
            flux = inverted(1, s, flux)
            block_m[s, pl.ds(2 * length, 2 * n), :] = flux
            if not last:
                picked[3 + s] = base_rows[3 + s] + folded(dot(same_m[...], side_by_side(flux)))

    def take_halos(par, last=False):
        for s in range(3):
            gap = DT * ENDO_GAP[s]
            value = jnp.concatenate([gap * halo_low[par, s], gap * halo_high[par, s]], axis=0)
            value = inverted(0, s, value)
            block_e[s, pl.ds(0, 2 * width), :] = value
            if not last:
                picked[s] += folded(dot(mix_e[...], side_by_side(value)))
            gap = DT * MUSC_GAP[s]
            span = pl.ds(s * length, length)
            value = jnp.concatenate(
                [gap * edge_left[par, span, :], gap * edge_right[par, span, :]], axis=0
            )
            value = inverted(1, s, value)
            block_m[s, pl.ds(0, 2 * length), :] = value
            if not last:
                picked[3 + s] += folded(dot(mix_m[...], side_by_side(value)))

    def endo_flux():
        flux = jnp.concatenate([block_e[s, pl.ds(2 * width, 2 * n), :] for s in range(3)], axis=1)
        return jnp.concatenate(halves(flux), axis=0)

    def flux_at_ends(nxt):
        flux = endo_flux()
        for first in (0, rows - width):
            span = pl.ds(first, width)
            gain = dot(put_e[span, :], flux)
            for s in range(3):
                endo[nxt, s, span, :] += gain[:, s * points:(s + 1) * points]

    def halo_at_ends(nxt):
        for s in range(3):
            endo[nxt, s, pl.ds(0, width), :] += block_e[s, pl.ds(0, width), :]
            endo[nxt, s, pl.ds(rows - width, width), :] += block_e[s, pl.ds(width, width), :]

    def finish_inside(nxt):
        span = pl.ds(width, rows - 2 * width)
        gain = dot(put_e[span, :], endo_flux())
        for s in range(3):
            endo[nxt, s, span, :] += gain[:, s * points:(s + 1) * points]

    def finish_musc(nxt):
        flux = jnp.concatenate([block_m[s, pl.ds(2 * length, 2 * n), :] for s in range(3)], axis=1)
        gain = dot(put_m[...], jnp.concatenate(halves(flux), axis=0))
        first = pl.ds(0, length, stride=cycle)
        final = pl.ds(cycle - 1, length, stride=cycle)
        for s in range(3):
            musc[nxt, s] += gain[:, s * points:(s + 1) * points]
            musc[nxt, s, first, :] = musc[nxt, s, first, :] + block_m[s, pl.ds(0, length), :]
            musc[nxt, s, final, :] = musc[nxt, s, final, :] + block_m[s, pl.ds(length, length), :]

    start_far(0)
    pack(0)
    launch(0)
    start_ends(0)
    start_sides(0)

    def step(t, carry):
        par = lax.rem(t, 2)
        nxt = 1 - par
        local_part(par, nxt, False)
        collect_messages(par)
        take_messages(par)
        flux_at_ends(nxt)
        collect_halos(par)
        take_halos(par)
        halo_at_ends(nxt)
        start_far(nxt)
        pl.when(t > 0)(lambda: messages(nxt).wait_send())
        pack(nxt)
        launch(nxt)
        start_ends(nxt)
        finish_musc(nxt)
        start_sides(nxt)
        finish_inside(nxt)
        return carry

    lax.fori_loop(0, TIME_STEPS - 1, step, 0)
    par = (TIME_STEPS - 1) % 2
    nxt = 1 - par
    local_part(par, nxt, True)
    collect_messages(par)
    take_messages(par, True)
    flux_at_ends(nxt)
    finish_inside(nxt)
    collect_halos(par)
    take_halos(par, True)
    halo_at_ends(nxt)
    store_e = pltpu.make_async_copy(endo.at[nxt], endo_out, in_sems.at[0])
    store_e.start()
    finish_musc(nxt)
    store_m = pltpu.make_async_copy(musc.at[nxt], musc_out, in_sems.at[1])
    store_m.start()
    messages(nxt).wait_send()
    messages(par).wait_send()
    store_e.wait()
    store_m.wait()


def hand_over(endo_from, musc_from, endo_to, musc_to, endo, musc, sems, out_sems):
    pairs = []
    for layer, (a, held, b) in enumerate(((endo_from, endo, endo_to), (musc_from, musc, musc_to))):
        for s in range(held.shape[0]):
            pairs.append((
                pltpu.make_async_copy(a.at[s], held.at[s], sems.at[layer, s]),
                pltpu.make_async_copy(held.at[s], b.at[s], out_sems.at[layer, s]),
            ))
    for load, store in pairs:
        load.start()
    for load, store in pairs:
        load.wait()
        store.start()
    for load, store in pairs:
        store.wait()


def local(
    n_ax, n_circ,
    endothelium, muscle, agonist, proj_cell, proj_target, proj_count, endo_inverse, muscle_inverse
):
    n = n_ax * n_circ
    species, endo_ax, width, points = endothelium.shape
    length, cycle = muscle.shape[1:3]
    rows = endo_ax * width
    musc_rows = length * cycle
    slots = proj_cell.shape[2]
    lane = jnp.arange(points, dtype=jnp.int32)[None, :]
    target, cell = proj_target[0], proj_cell[0]
    live = lane % slots < proj_count[0][:, None]
    first = jnp.where(lane == 0, target[:, 0:1], target[:, 1:2])
    second = jnp.where(lane == slots, cell[:, 0:1], cell[:, 1:2])
    meta = jnp.where(live, jnp.where(lane < slots, first, second), rows + musc_rows)
    anywhere = pl.BlockSpec(memory_space=pl.ANY)
    dma = pltpu.SemaphoreType.DMA
    body = functools.partial(kernel, (n_ax, n_circ, width, length, cycle))
    endo_next, musc_next = pl.pallas_call(
        body,
        out_shape=(
            jax.ShapeDtypeStruct((species, rows, points), F32),
            jax.ShapeDtypeStruct((species, musc_rows, points), F32),
        ),
        in_specs=[anywhere] * 6,
        out_specs=(anywhere, anywhere),
        scratch_shapes=[
            pltpu.VMEM((2, species, rows, points), F32),
            pltpu.VMEM((2, species, musc_rows, points), F32),
            pltpu.VMEM((2, species, width, points), F32),
            pltpu.VMEM((2, species, width, points), F32),
            pltpu.VMEM((2, species * length, points), F32),
            pltpu.VMEM((2, species * length, points), F32),
            pltpu.VMEM((2, species * length, points), F32),
            pltpu.VMEM((2, n, 16, points), F32),
            pltpu.VMEM((2, n, 16, points), F32),
            pltpu.VMEM((6, slots * n, points), F32),
            pltpu.VMEM((6, slots * n, points), F32),
            pltpu.VMEM((6, 2 * points, 2 * points), BF16),
            pltpu.VMEM((slots * n, rows), BF16),
            pltpu.VMEM((slots * n, musc_rows), BF16),
            pltpu.VMEM((rows, 2 * slots * n), BF16),
            pltpu.VMEM((musc_rows, 2 * slots * n), BF16),
            pltpu.VMEM((slots * n, 2 * width), BF16),
            pltpu.VMEM((slots * n, 2 * length), BF16),
            pltpu.VMEM((slots * n, slots * n), BF16),
            pltpu.VMEM((slots * n, slots * n), BF16),
            pltpu.VMEM((6, max(rows, musc_rows), 2 * points), BF16),
            pltpu.VMEM((species, 2 * width + slots * n, points), F32),
            pltpu.VMEM((species, 2 * length + slots * n, points), F32),
            pltpu.VMEM((rows, points), F32),
            pltpu.VMEM((n, 1, points), jnp.int32),
            pltpu.VMEM((n, 1, points), jnp.int32),
            pltpu.VMEM((species, points, points), F32),
            pltpu.VMEM((species, points, points), F32),
            dma((6,)), dma, dma((2,)), dma((2,)),
            dma((2,)), dma((2, 2)), dma((2,)), dma((2, 2)),
            dma((2,)),
            pltpu.VMEM((2, 2, species, width - width // 2, points), F32),
            dma((2, 2)), dma((2,)),
        ],
        compiler_params=pltpu.CompilerParams(
            collective_id=0, has_side_effects=True, vmem_limit_bytes=60 * 1024 * 1024
        ),
        name="cable_steps",
    )(
        endothelium.reshape(species, rows, points),
        muscle.reshape(species, musc_rows, points),
        agonist.reshape(rows, points),
        meta[:, None, :],
        endo_inverse, muscle_inverse,
    )
    endo_next, musc_next = pl.pallas_call(
        hand_over,
        out_shape=(
            jax.ShapeDtypeStruct((species, rows, points), F32),
            jax.ShapeDtypeStruct((species, musc_rows, points), F32),
        ),
        in_specs=[anywhere] * 2,
        out_specs=(anywhere, anywhere),
        scratch_shapes=[
            pltpu.VMEM((species, rows, points), F32),
            pltpu.VMEM((species, musc_rows, points), F32),
            dma((2, species)), dma((2, species)),
        ],
        compiler_params=pltpu.CompilerParams(vmem_limit_bytes=60 * 1024 * 1024),
        name="hand_over",
    )(endo_next, musc_next)
    return endo_next.reshape(endothelium.shape), musc_next.reshape(muscle.shape)


def solution(mesh):
    tiles = P(None, "ax", "circ", None)
    sent = P(("ax", "circ"), None, None)
    return jax.shard_map(
        functools.partial(local, mesh.shape["ax"], mesh.shape["circ"]),
        mesh=mesh,
        in_specs=(tiles, tiles, P("ax", "circ", None), sent, sent, P(("ax", "circ"), None), P(), P()),
        out_specs=(tiles, tiles),
        check_vma=False,
    )
```

```python
import functools

import jax
import jax.numpy as jnp
from jax import lax
from jax.experimental import pallas as pl
from jax.experimental.pallas import tpu as pltpu
from jax.sharding import PartitionSpec as P

MESH = pl.DeviceIdType.MESH
TIME_STEPS = 8
DT = 0.2
COUPLING = (0.1, 0.3, 0.5)
ENDO_GAP = (0.05, 0.3, 0.5)
MUSC_GAP = (0.05, 0.1, 0.4)
BF16 = jnp.bfloat16
F32 = jnp.float32


def halves(x):
    high = x.astype(BF16)
    return high, (x - high.astype(F32)).astype(BF16)


def side_by_side(x):
    return jnp.concatenate(halves(x), axis=1)


def folded(y):
    half = y.shape[1] // 2
    return y[:, :half] + y[:, half:]


def dot(a, b):
    return jnp.dot(a, b, preferred_element_type=F32)


def reaction(u0, u1, u2, drive):
    square = u1 * u1
    release = square / (0.5 + square)
    second = -0.5 * u1 if drive is None else drive - 0.5 * u1
    return (1.2 * release - 0.6 * u0 - 0.2 * u2, second, 0.5 * u0 - 0.8 * u2)


def kernel(
    sizes,
    endo_in, musc_in, agonist_in, target_in, cell_in, count_in, endo_inv_in, musc_inv_in,
    endo_out, musc_out,
    endo, musc, halo_low, halo_high, edge_out, edge_left, edge_right,
    send, recv, picked, base_rows, weights, take_e, take_m, put_e, put_m, mix_e, mix_m, same_e, same_m, rhs,
    block_e, block_m, agonist, meta, meta_recv, endo_inv, musc_inv, targets, starts_at, counts,
    in_sems, own_sem, send_sem, recv_sem, halo_send, halo_recv, edge_send, edge_recv,
    meta_sems, relay, relay_recv, relay_send,
):
    n_ax, n_circ, width, length, cycle = sizes
    n = n_ax * n_circ
    points = endo.shape[3]
    rows = endo.shape[2]
    musc_rows = musc.shape[2]
    ax = lax.axis_index("ax")
    circ = lax.axis_index("circ")
    me = ax * n_circ + circ
    right = lax.rem(circ + 1, n_circ)
    left = lax.rem(circ + n_circ - 1, n_circ)
    half = width // 2
    corners = n_ax % 4 == 0 and n_ax > 4
    turn = lax.rem(ax, 4)
    up_far = (turn == 3) & (ax < n_ax - 1)
    down_far = (turn == 0) & (ax > 0)
    relay_up = (turn == 3) & (ax > 3)
    relay_down = (turn == 0) & (ax < n_ax - 4)
    turned = [lax.rem(circ + c, n_circ) for c in range(n_circ)]

    def each_peer(act):
        def some(j, carry):
            far = lax.rem(ax + j, n_ax)
            for c in reversed(range(n_circ)):
                act(far, turned[c])
            return carry

        lax.fori_loop(1, n_ax, some, 0)
        for c in reversed(range(1, n_circ)):
            act(ax, turned[c])

    loads = [
        pltpu.make_async_copy(a, b, in_sems.at[i])
        for i, (a, b) in enumerate(
            (
                (target_in, targets), (endo_in, endo.at[0]), (musc_in, musc.at[0]),
                (endo_inv_in, endo_inv), (musc_inv_in, musc_inv), (agonist_in, agonist),
                (cell_in, starts_at), (count_in, counts),
            )
        )
    ]
    for load in loads:
        load.start()

    barrier = pltpu.get_barrier_semaphore()

    def greet(pa, pc):
        pl.semaphore_signal(barrier, inc=1, device_id=(pa, pc), device_id_type=MESH)

    each_peer(greet)

    @pl.when(ax == 0)
    def _():
        halo_low[...] = jnp.zeros_like(halo_low)

    @pl.when(ax == n_ax - 1)
    def _():
        halo_high[...] = jnp.zeros_like(halo_high)

    for i in (0, 6, 7):
        loads[i].wait()
    live = lax.broadcasted_iota(jnp.int32, targets.shape, 0) < counts[...]
    nowhere = rows + musc_rows
    table = jnp.concatenate(
        [
            jnp.where(live, targets[...], nowhere).astype(F32),
            jnp.where(live, starts_at[...], nowhere).astype(F32),
            jnp.zeros((4, n), F32),
        ],
        axis=0,
    )
    if n % 128:
        table = jnp.concatenate([table, jnp.zeros((8, 128 - n % 128), F32)], axis=1)
    columns = table.T[:n]
    meta[:, 0, :] = jnp.concatenate(
        [columns, jnp.zeros((n, points - 8), F32)], axis=1
    ).astype(jnp.int32)
    pl.semaphore_wait(barrier, n - 1)

    def cells(par, from_top, start, count):
        first = rows - width if from_top else 0
        return endo.at[par, :, pl.ds(first + start, count)]

    def end_copy(par, up, start, count):
        dst = halo_low if up else halo_high
        return pltpu.make_async_remote_copy(
            src_ref=cells(par, up, start, count), dst_ref=dst.at[par, :, pl.ds(start, count)],
            send_sem=halo_send.at[int(up)], recv_sem=halo_recv.at[par, int(up)],
            device_id=(ax + 1 if up else ax - 1, circ), device_id_type=MESH,
        )

    def to_relay(par, up):
        return pltpu.make_async_remote_copy(
            src_ref=cells(par, up, half, width - half), dst_ref=relay.at[par, int(up)],
            send_sem=halo_send.at[int(up)], recv_sem=relay_recv.at[par, int(up)],
            device_id=(ax + 4 if up else ax - 4, circ), device_id_type=MESH,
        )

    def from_relay(par, up):
        dst = halo_low if up else halo_high
        return pltpu.make_async_remote_copy(
            src_ref=relay.at[par, int(up)], dst_ref=dst.at[par, :, pl.ds(half, width - half)],
            send_sem=relay_send.at[int(up)], recv_sem=halo_recv.at[par, int(up)],
            device_id=(ax - 3 if up else ax + 3, circ), device_id_type=MESH,
        )

    def start_far(par):
        if corners:
            pl.when(up_far)(to_relay(par, True).start)
            pl.when(down_far)(to_relay(par, False).start)

    def start_ends(par):
        if corners:
            pl.when(up_far)(end_copy(par, True, 0, half).start)
            pl.when(down_far)(end_copy(par, False, 0, half).start)
            pl.when((ax < n_ax - 1) & (turn != 3))(end_copy(par, True, 0, width).start)
            pl.when((ax > 0) & (turn != 0))(end_copy(par, False, 0, width).start)
        else:
            pl.when(ax < n_ax - 1)(end_copy(par, True, 0, width).start)
            pl.when(ax > 0)(end_copy(par, False, 0, width).start)

    def tell(pa, pc):
        pltpu.make_async_remote_copy(
            src_ref=meta.at[pa * n_circ + pc], dst_ref=meta_recv.at[me],
            send_sem=meta_sems.at[0], recv_sem=meta_sems.at[1],
            device_id=(pa, pc), device_id_type=MESH,
        ).start()

    each_peer(tell)
    loads[1].wait()
    start_far(0)
    start_ends(0)
    own_meta = pltpu.make_async_copy(meta.at[me], meta_recv.at[me], own_sem)
    own_meta.start()

    loads[3].wait()
    loads[4].wait()
    for layer, inv in ((0, endo_inv), (1, musc_inv)):
        for s in range(3):
            row = side_by_side(inv[s].T)
            weights[layer * 3 + s] = jnp.concatenate([row, row], axis=0)

    def choose(ids, take, put):
        cells = lax.broadcasted_iota(jnp.int32, take.shape, 1)
        chosen = jnp.where(cells == ids, 1.0, 0.0)
        take[...] = chosen.astype(BF16)
        spread = chosen.T
        put[...] = jnp.concatenate([spread, spread], axis=1).astype(BF16)
        return chosen, dot(chosen.astype(BF16), spread.astype(BF16))

    sent = meta[:, 0, :]
    ids = jnp.concatenate([sent[:, 2:3], sent[:, 3:4]], axis=0)
    chosen, same = choose(ids, take_e, put_e)
    mix_e[...] = jnp.concatenate([chosen[:, :width], chosen[:, rows - width:]], axis=1).astype(BF16)
    same_e[...] = same.astype(BF16)

    def gather(layer, s, values, out):
        take = take_e if layer == 0 else take_m
        out[layer * 3 + s] = folded(dot(take[...], side_by_side(values)))

    loads[2].wait()
    loads[5].wait()
    for s in range(3):
        gather(0, s, endo[0, s], picked)

    told = pltpu.make_async_remote_copy(
        src_ref=meta.at[pl.ds(0, n - 1)], dst_ref=meta_recv.at[pl.ds(0, n - 1)],
        send_sem=meta_sems.at[0], recv_sem=meta_sems.at[1],
        device_id=(ax, right), device_id_type=MESH,
    )
    told.wait_recv()
    own_meta.wait()
    got = meta_recv[:, 0, :]
    ids = jnp.concatenate([got[:, 0:1], got[:, 1:2]], axis=0)
    chosen, same = choose(ids, take_m, put_m)
    starts = lax.broadcasted_iota(jnp.int32, (ids.shape[0], length), 1) * cycle
    mix_m[...] = jnp.concatenate(
        [
            jnp.where(starts == ids, 1.0, 0.0),
            jnp.where(starts + (cycle - 1) == ids, 1.0, 0.0),
        ],
        axis=1,
    ).astype(BF16)
    same_m[...] = same.astype(BF16)
    for s in range(3):
        gather(1, s, musc[0, s], picked)
    told.wait_send()

    def messages(par):
        return pltpu.make_async_remote_copy(
            src_ref=send.at[par, pl.ds(0, n - 1), pl.ds(0, 12)],
            dst_ref=recv.at[par, pl.ds(0, n - 1), pl.ds(0, 12)],
            send_sem=send_sem.at[par], recv_sem=recv_sem.at[par],
            device_id=(ax, right), device_id_type=MESH,
        )

    def own_copy(par):
        return pltpu.make_async_copy(
            send.at[par, me, pl.ds(0, 12)], recv.at[par, me, pl.ds(0, 12)], own_sem
        )

    def pack(par):
        flat = send.at[par].reshape(n * 16, points)
        for q in range(6):
            for slot in range(2):
                flat[pl.ds(q * 2 + slot, n, stride=16), :] = picked[q, pl.ds(slot * n, n), :]

    def launch(par):
        def post(pa, pc):
            pltpu.make_async_remote_copy(
                src_ref=send.at[par, pa * n_circ + pc, pl.ds(0, 12)],
                dst_ref=recv.at[par, me, pl.ds(0, 12)],
                send_sem=send_sem.at[par],
                recv_sem=recv_sem.at[par],
                device_id=(pa, pc),
                device_id_type=MESH,
            ).start()

        each_peer(post)
        own_copy(par).start()

    def pass_on(par):
        if not corners:
            return
        for up, here in ((True, relay_up), (False, relay_down)):

            @pl.when(here)
            def _():
                to_relay(par, up).wait_recv()
                from_relay(par, up).start()

    def passed_on(par):
        if corners:
            pl.when(relay_up)(from_relay(par, True).wait_send)
            pl.when(relay_down)(from_relay(par, False).wait_send)

    def sides(par):
        to_left = pltpu.make_async_remote_copy(
            src_ref=edge_out.at[0], dst_ref=edge_right.at[par],
            send_sem=edge_send.at[0], recv_sem=edge_recv.at[par, 0],
            device_id=(ax, left), device_id_type=MESH,
        )
        to_right = pltpu.make_async_remote_copy(
            src_ref=edge_out.at[1], dst_ref=edge_left.at[par],
            send_sem=edge_send.at[1], recv_sem=edge_recv.at[par, 1],
            device_id=(ax, right), device_id_type=MESH,
        )
        return to_left, to_right

    def start_sides(par):
        for s in range(3):
            span = pl.ds(s * length, length)
            edge_out[0, span] = musc[par, s, pl.ds(0, length, stride=cycle), :]
            edge_out[1, span] = musc[par, s, pl.ds(cycle - 1, length, stride=cycle), :]
        for copy in sides(par):
            copy.start()

    def local_part(par, nxt, last):
        count = rows // width
        for a in range(count):
            for j in range(0, width, 64):
                here = pl.ds(a * width + j, 64)
                u = [endo[par, s, here, :] for s in range(3)]
                parts = reaction(u[0], u[1], u[2], agonist[here, :])
                for s in range(3):
                    lap = -2.0 * u[s]
                    if a > 0:
                        lap = lap + endo[par, s, pl.ds((a - 1) * width + j, 64), :]
                    if a < count - 1:
                        lap = lap + endo[par, s, pl.ds((a + 1) * width + j, 64), :]
                    value = u[s] + DT * (parts[s] + ENDO_GAP[s] * lap)
                    rhs[s, here, :] = side_by_side(value)

        pass_on(par)

        def musc_base(a, carry):
            here = pl.ds(pl.multiple_of(a * cycle, cycle), cycle)
            place_in = lax.broadcasted_iota(jnp.int32, (cycle, points), 0)
            u = [musc[par, s, here, :] for s in range(3)]
            parts = reaction(u[0], u[1], u[2], None)
            for s in range(3):
                before = jnp.where(place_in == 0, 0.0, pltpu.roll(u[s], 1, 0))
                after = jnp.where(place_in == cycle - 1, 0.0, pltpu.roll(u[s], cycle - 1, 0))
                lap = before + after - 2.0 * u[s]
                value = u[s] + DT * (parts[s] + MUSC_GAP[s] * lap)
                rhs[3 + s, here, :] = side_by_side(value)
            return carry

        lax.fori_loop(0, length, musc_base, 0)

        for layer, state in ((0, endo), (1, musc)):
            for s in range(3):
                value = folded(dot(rhs[layer * 3 + s], weights[layer * 3 + s]))
                state[nxt, s] = value
                if not last:
                    gather(layer, s, value, base_rows)

    def collect_messages(par):
        own_copy(par).wait()
        messages(par).wait_recv()

    def collect_halos(par):
        for copy in sides(par):
            copy.wait()
        passed_on(par)

        @pl.when(ax > 0)
        def _():
            end_copy(par, False, 0, width).wait_send()
            end_copy(par, True, 0, width).wait_recv()

        @pl.when(ax < n_ax - 1)
        def _():
            end_copy(par, True, 0, width).wait_send()
            end_copy(par, False, 0, width).wait_recv()

    def arrived(par, layer, s):
        flat = recv.at[par].reshape(n * 16, points)
        k = layer * 6 + s * 2
        return jnp.concatenate(
            [flat[pl.ds(k + slot, n, stride=16), :] for slot in range(2)], axis=0
        )

    def inverted(layer, s, value):
        return folded(dot(side_by_side(value), weights[layer * 3 + s]))

    def take_messages(par, last=False):
        for s in range(3):
            flux = (DT * COUPLING[s]) * (arrived(par, 1, s) - picked[s])
            flux = inverted(0, s, flux)
            block_e[s, pl.ds(2 * width, 2 * n), :] = flux
            if not last:
                picked[s] = base_rows[s] + folded(dot(same_e[...], side_by_side(flux)))
            flux = (DT * COUPLING[s]) * (arrived(par, 0, s) - picked[3 + s])
            flux = inverted(1, s, flux)
            block_m[s, pl.ds(2 * length, 2 * n), :] = flux
            if not last:
                picked[3 + s] = base_rows[3 + s] + folded(dot(same_m[...], side_by_side(flux)))

    def take_halos(par, last=False):
        for s in range(3):
            gap = DT * ENDO_GAP[s]
            value = jnp.concatenate([gap * halo_low[par, s], gap * halo_high[par, s]], axis=0)
            value = inverted(0, s, value)
            block_e[s, pl.ds(0, 2 * width), :] = value
            if not last:
                picked[s] += folded(dot(mix_e[...], side_by_side(value)))
            gap = DT * MUSC_GAP[s]
            span = pl.ds(s * length, length)
            value = jnp.concatenate(
                [gap * edge_left[par, span, :], gap * edge_right[par, span, :]], axis=0
            )
            value = inverted(1, s, value)
            block_m[s, pl.ds(0, 2 * length), :] = value
            if not last:
                picked[3 + s] += folded(dot(mix_m[...], side_by_side(value)))

    def endo_flux():
        flux = jnp.concatenate([block_e[s, pl.ds(2 * width, 2 * n), :] for s in range(3)], axis=1)
        return jnp.concatenate(halves(flux), axis=0)

    def flux_at_ends(nxt):
        flux = endo_flux()
        for first in (0, rows - width):
            span = pl.ds(first, width)
            gain = dot(put_e[span, :], flux)
            for s in range(3):
                endo[nxt, s, span, :] += gain[:, s * points:(s + 1) * points]

    def halo_at_ends(nxt):
        for s in range(3):
            endo[nxt, s, pl.ds(0, width), :] += block_e[s, pl.ds(0, width), :]
            endo[nxt, s, pl.ds(rows - width, width), :] += block_e[s, pl.ds(width, width), :]

    def finish_inside(nxt):
        span = pl.ds(width, rows - 2 * width)
        gain = dot(put_e[span, :], endo_flux())
        for s in range(3):
            endo[nxt, s, span, :] += gain[:, s * points:(s + 1) * points]

    def finish_musc(nxt):
        flux = jnp.concatenate([block_m[s, pl.ds(2 * length, 2 * n), :] for s in range(3)], axis=1)
        gain = dot(put_m[...], jnp.concatenate(halves(flux), axis=0))
        first = pl.ds(0, length, stride=cycle)
        final = pl.ds(cycle - 1, length, stride=cycle)
        for s in range(3):
            musc[nxt, s] += gain[:, s * points:(s + 1) * points]
            musc[nxt, s, first, :] = musc[nxt, s, first, :] + block_m[s, pl.ds(0, length), :]
            musc[nxt, s, final, :] = musc[nxt, s, final, :] + block_m[s, pl.ds(length, length), :]

    start_sides(0)
    pack(0)
    launch(0)

    def step(t, carry):
        par = lax.rem(t, 2)
        nxt = 1 - par
        local_part(par, nxt, False)
        collect_messages(par)
        take_messages(par)
        flux_at_ends(nxt)
        collect_halos(par)
        take_halos(par)
        halo_at_ends(nxt)
        start_far(nxt)
        start_ends(nxt)
        pl.when(t > 0)(lambda: messages(nxt).wait_send())
        pack(nxt)
        launch(nxt)
        finish_musc(nxt)
        start_sides(nxt)
        finish_inside(nxt)
        return carry

    lax.fori_loop(0, TIME_STEPS - 1, step, 0)
    par = (TIME_STEPS - 1) % 2
    nxt = 1 - par
    local_part(par, nxt, True)
    collect_messages(par)
    take_messages(par, True)
    flux_at_ends(nxt)
    finish_inside(nxt)
    collect_halos(par)
    take_halos(par, True)
    halo_at_ends(nxt)
    store_e = pltpu.make_async_copy(endo.at[nxt], endo_out, in_sems.at[0])
    store_e.start()
    finish_musc(nxt)
    store_m = pltpu.make_async_copy(musc.at[nxt], musc_out, in_sems.at[1])
    store_m.start()
    messages(nxt).wait_send()
    messages(par).wait_send()
    store_e.wait()
    store_m.wait()


def hand_over(endo_from, musc_from, endo_to, musc_to, endo, musc, sems, out_sems):
    pairs = []
    for layer, (a, held, b) in enumerate(((endo_from, endo, endo_to), (musc_from, musc, musc_to))):
        for s in range(held.shape[0]):
            pairs.append((
                pltpu.make_async_copy(a.at[s], held.at[s], sems.at[layer, s]),
                pltpu.make_async_copy(held.at[s], b.at[s], out_sems.at[layer, s]),
            ))
    for load, store in pairs:
        load.start()
    for load, store in pairs:
        load.wait()
        store.start()
    for load, store in pairs:
        store.wait()


def local(
    n_ax, n_circ,
    endothelium, muscle, agonist, proj_cell, proj_target, proj_count, endo_inverse, muscle_inverse
):
    n = n_ax * n_circ
    species, endo_ax, width, points = endothelium.shape
    length, cycle = muscle.shape[1:3]
    rows = endo_ax * width
    musc_rows = length * cycle
    slots = proj_cell.shape[2]
    anywhere = pl.BlockSpec(memory_space=pl.ANY)
    dma = pltpu.SemaphoreType.DMA
    body = functools.partial(kernel, (n_ax, n_circ, width, length, cycle))
    endo_next, musc_next = pl.pallas_call(
        body,
        out_shape=(
            jax.ShapeDtypeStruct((species, rows, points), F32),
            jax.ShapeDtypeStruct((species, musc_rows, points), F32),
        ),
        in_specs=[anywhere] * 8,
        out_specs=(anywhere, anywhere),
        scratch_shapes=[
            pltpu.VMEM((2, species, rows, points), F32),
            pltpu.VMEM((2, species, musc_rows, points), F32),
            pltpu.VMEM((2, species, width, points), F32),
            pltpu.VMEM((2, species, width, points), F32),
            pltpu.VMEM((2, species * length, points), F32),
            pltpu.VMEM((2, species * length, points), F32),
            pltpu.VMEM((2, species * length, points), F32),
            pltpu.VMEM((2, n, 16, points), F32),
            pltpu.VMEM((2, n, 16, points), F32),
            pltpu.VMEM((6, slots * n, points), F32),
            pltpu.VMEM((6, slots * n, points), F32),
            pltpu.VMEM((6, 2 * points, 2 * points), BF16),
            pltpu.VMEM((slots * n, rows), BF16),
            pltpu.VMEM((slots * n, musc_rows), BF16),
            pltpu.VMEM((rows, 2 * slots * n), BF16),
            pltpu.VMEM((musc_rows, 2 * slots * n), BF16),
            pltpu.VMEM((slots * n, 2 * width), BF16),
            pltpu.VMEM((slots * n, 2 * length), BF16),
            pltpu.VMEM((slots * n, slots * n), BF16),
            pltpu.VMEM((slots * n, slots * n), BF16),
            pltpu.VMEM((6, max(rows, musc_rows), 2 * points), BF16),
            pltpu.VMEM((species, 2 * width + slots * n, points), F32),
            pltpu.VMEM((species, 2 * length + slots * n, points), F32),
            pltpu.VMEM((rows, points), F32),
            pltpu.VMEM((n, 1, points), jnp.int32),
            pltpu.VMEM((n, 1, points), jnp.int32),
            pltpu.VMEM((species, points, points), F32),
            pltpu.VMEM((species, points, points), F32),
            pltpu.VMEM((slots, n), jnp.int32),
            pltpu.VMEM((slots, n), jnp.int32),
            pltpu.VMEM((1, n), jnp.int32),
            dma((8,)), dma, dma((2,)), dma((2,)),
            dma((2,)), dma((2, 2)), dma((2,)), dma((2, 2)),
            dma((2,)),
            pltpu.VMEM((2, 2, species, width - width // 2, points), F32),
            dma((2, 2)), dma((2,)),
        ],
        compiler_params=pltpu.CompilerParams(
            collective_id=0, has_side_effects=True, vmem_limit_bytes=60 * 1024 * 1024
        ),
        name="cable_steps",
    )(
        endothelium.reshape(species, rows, points),
        muscle.reshape(species, musc_rows, points),
        agonist.reshape(rows, points),
        proj_target[0].T, proj_cell[0].T, proj_count,
        endo_inverse, muscle_inverse,
    )
    endo_next, musc_next = pl.pallas_call(
        hand_over,
        out_shape=(
            jax.ShapeDtypeStruct((species, rows, points), F32),
            jax.ShapeDtypeStruct((species, musc_rows, points), F32),
        ),
        in_specs=[anywhere] * 2,
        out_specs=(anywhere, anywhere),
        scratch_shapes=[
            pltpu.VMEM((species, rows, points), F32),
            pltpu.VMEM((species, musc_rows, points), F32),
            dma((2, species)), dma((2, species)),
        ],
        compiler_params=pltpu.CompilerParams(vmem_limit_bytes=60 * 1024 * 1024),
        name="hand_over",
    )(endo_next, musc_next)
    return endo_next.reshape(endothelium.shape), musc_next.reshape(muscle.shape)


def solution(mesh):
    tiles = P(None, "ax", "circ", None)
    sent = P(("ax", "circ"), None, None)
    return jax.shard_map(
        functools.partial(local, mesh.shape["ax"], mesh.shape["circ"]),
        mesh=mesh,
        in_specs=(tiles, tiles, P("ax", "circ", None), sent, sent, P(("ax", "circ"), None), P(), P()),
        out_specs=(tiles, tiles),
        check_vma=False,
    )
```

```python
import functools

import jax
import jax.numpy as jnp
from jax import lax
from jax.experimental import pallas as pl
from jax.experimental.pallas import tpu as pltpu
from jax.sharding import PartitionSpec as P

MESH = pl.DeviceIdType.MESH
TIME_STEPS = 8
DT = 0.2
COUPLING = (0.1, 0.3, 0.5)
ENDO_GAP = (0.05, 0.3, 0.5)
MUSC_GAP = (0.05, 0.1, 0.4)
BF16 = jnp.bfloat16
F32 = jnp.float32


def halves(x):
    high = x.astype(BF16)
    return high, (x - high.astype(F32)).astype(BF16)


def side_by_side(x):
    return jnp.concatenate(halves(x), axis=1)


def folded(y):
    half = y.shape[1] // 2
    return y[:, :half] + y[:, half:]


def dot(a, b):
    return jnp.dot(a, b, preferred_element_type=F32)


def reaction(u0, u1, u2, drive):
    square = u1 * u1
    release = square / (0.5 + square)
    second = -0.5 * u1 if drive is None else drive - 0.5 * u1
    return (1.2 * release - 0.6 * u0 - 0.2 * u2, second, 0.5 * u0 - 0.8 * u2)


def kernel(
    sizes,
    endo_in, musc_in, agonist_in, target_in, cell_in, count_in, endo_inv_in, musc_inv_in,
    endo_out, musc_out,
    endo, musc, halo_low, halo_high, edge_out, edge_left, edge_right,
    send, recv, picked, base_rows, weights, take_e, take_m, put_e, put_m, mix_e, mix_m, rhs,
    block_e, block_m, agonist, meta, meta_recv, endo_inv, musc_inv, targets, starts_at, counts,
    in_sems, own_sem, send_sem, recv_sem, halo_send, halo_recv, edge_send, edge_recv,
    meta_sems, relay, relay_recv, relay_send,
):
    n_ax, n_circ, width, length, cycle = sizes
    n = n_ax * n_circ
    points = endo.shape[3]
    rows = endo.shape[2]
    musc_rows = musc.shape[2]
    ax = lax.axis_index("ax")
    circ = lax.axis_index("circ")
    me = ax * n_circ + circ
    right = lax.rem(circ + 1, n_circ)
    left = lax.rem(circ + n_circ - 1, n_circ)
    half = width // 2
    corners = n_ax % 4 == 0 and n_ax > 4
    turn = lax.rem(ax, 4)
    up_far = (turn == 3) & (ax < n_ax - 1)
    down_far = (turn == 0) & (ax > 0)
    relay_up = (turn == 3) & (ax > 3)
    relay_down = (turn == 0) & (ax < n_ax - 4)
    turned = [lax.rem(circ + c, n_circ) for c in range(n_circ)]

    def each_peer(act):
        def some(j, carry):
            far = lax.rem(ax + j, n_ax)
            for c in reversed(range(n_circ)):
                act(far, turned[c])
            return carry

        lax.fori_loop(1, n_ax, some, 0)
        for c in reversed(range(1, n_circ)):
            act(ax, turned[c])

    loads = [
        pltpu.make_async_copy(a, b, in_sems.at[i])
        for i, (a, b) in enumerate(
            (
                (target_in, targets), (endo_in, endo.at[0]), (musc_in, musc.at[0]),
                (endo_inv_in, endo_inv), (musc_inv_in, musc_inv), (agonist_in, agonist),
                (cell_in, starts_at), (count_in, counts),
            )
        )
    ]
    for load in loads:
        load.start()

    barrier = pltpu.get_barrier_semaphore()

    def greet(pa, pc):
        pl.semaphore_signal(barrier, inc=1, device_id=(pa, pc), device_id_type=MESH)

    each_peer(greet)

    @pl.when(ax == 0)
    def _():
        halo_low[...] = jnp.zeros_like(halo_low)

    @pl.when(ax == n_ax - 1)
    def _():
        halo_high[...] = jnp.zeros_like(halo_high)

    for i in (0, 6, 7):
        loads[i].wait()
    live = lax.broadcasted_iota(jnp.int32, targets.shape, 0) < counts[...]
    nowhere = rows + musc_rows
    table = jnp.concatenate(
        [
            jnp.where(live, targets[...], nowhere).astype(F32),
            jnp.where(live, starts_at[...], nowhere).astype(F32),
            jnp.zeros((4, n), F32),
        ],
        axis=0,
    )
    if n % 128:
        table = jnp.concatenate([table, jnp.zeros((8, 128 - n % 128), F32)], axis=1)
    columns = table.T[:n]
    meta[:, 0, :] = jnp.concatenate(
        [columns, jnp.zeros((n, points - 8), F32)], axis=1
    ).astype(jnp.int32)
    pl.semaphore_wait(barrier, n - 1)

    def tell(pa, pc):
        pltpu.make_async_remote_copy(
            src_ref=meta.at[pa * n_circ + pc], dst_ref=meta_recv.at[me],
            send_sem=meta_sems.at[0], recv_sem=meta_sems.at[1],
            device_id=(pa, pc), device_id_type=MESH,
        ).start()

    each_peer(tell)
    own_meta = pltpu.make_async_copy(meta.at[me], meta_recv.at[me], own_sem)
    own_meta.start()

    loads[3].wait()
    loads[4].wait()
    for layer, inv in ((0, endo_inv), (1, musc_inv)):
        for s in range(3):
            row = side_by_side(inv[s].T)
            weights[layer * 3 + s] = jnp.concatenate([row, row], axis=0)

    def choose(ids, take, put):
        cells = lax.broadcasted_iota(jnp.int32, take.shape, 1)
        chosen = jnp.where(cells == ids, 1.0, 0.0)
        take[...] = chosen.astype(BF16)
        spread = chosen.T
        put[...] = jnp.concatenate([spread, spread], axis=1).astype(BF16)
        return chosen, dot(chosen.astype(BF16), spread.astype(BF16))

    sent = meta[:, 0, :]
    ids = jnp.concatenate([sent[:, 2:3], sent[:, 3:4]], axis=0)
    chosen, same = choose(ids, take_e, put_e)
    mix_e[...] = jnp.concatenate(
        [chosen[:, :width], chosen[:, rows - width:], same], axis=1
    ).astype(BF16)

    def gather(layer, s, values, out):
        take = take_e if layer == 0 else take_m
        out[layer * 3 + s] = folded(dot(take[...], side_by_side(values)))

    loads[1].wait()
    loads[2].wait()
    loads[5].wait()
    for s in range(3):
        gather(0, s, endo[0, s], picked)

    told = pltpu.make_async_remote_copy(
        src_ref=meta.at[pl.ds(0, n - 1)], dst_ref=meta_recv.at[pl.ds(0, n - 1)],
        send_sem=meta_sems.at[0], recv_sem=meta_sems.at[1],
        device_id=(ax, right), device_id_type=MESH,
    )
    told.wait_recv()
    own_meta.wait()
    got = meta_recv[:, 0, :]
    ids = jnp.concatenate([got[:, 0:1], got[:, 1:2]], axis=0)
    chosen, same = choose(ids, take_m, put_m)
    starts = lax.broadcasted_iota(jnp.int32, (ids.shape[0], length), 1) * cycle
    mix_m[...] = jnp.concatenate(
        [
            jnp.where(starts == ids, 1.0, 0.0),
            jnp.where(starts + (cycle - 1) == ids, 1.0, 0.0),
            same,
        ],
        axis=1,
    ).astype(BF16)
    for s in range(3):
        gather(1, s, musc[0, s], picked)
    told.wait_send()

    def messages(par):
        return pltpu.make_async_remote_copy(
            src_ref=send.at[par, pl.ds(0, n - 1), pl.ds(0, 12)],
            dst_ref=recv.at[par, pl.ds(0, n - 1), pl.ds(0, 12)],
            send_sem=send_sem.at[par], recv_sem=recv_sem.at[par],
            device_id=(ax, right), device_id_type=MESH,
        )

    def own_copy(par):
        return pltpu.make_async_copy(
            send.at[par, me, pl.ds(0, 12)], recv.at[par, me, pl.ds(0, 12)], own_sem
        )

    def pack(par):
        flat = send.at[par].reshape(n * 16, points)
        for q in range(6):
            for slot in range(2):
                flat[pl.ds(q * 2 + slot, n, stride=16), :] = picked[q, pl.ds(slot * n, n), :]

    def launch(par):
        def post(pa, pc):
            pltpu.make_async_remote_copy(
                src_ref=send.at[par, pa * n_circ + pc, pl.ds(0, 12)],
                dst_ref=recv.at[par, me, pl.ds(0, 12)],
                send_sem=send_sem.at[par],
                recv_sem=recv_sem.at[par],
                device_id=(pa, pc),
                device_id_type=MESH,
            ).start()

        each_peer(post)
        own_copy(par).start()

    def cells(par, from_top, start, count):
        first = rows - width if from_top else 0
        return endo.at[par, :, pl.ds(first + start, count)]

    def end_copy(par, up, start, count):
        dst = halo_low if up else halo_high
        return pltpu.make_async_remote_copy(
            src_ref=cells(par, up, start, count), dst_ref=dst.at[par, :, pl.ds(start, count)],
            send_sem=halo_send.at[int(up)], recv_sem=halo_recv.at[par, int(up)],
            device_id=(ax + 1 if up else ax - 1, circ), device_id_type=MESH,
        )

    def to_relay(par, up):
        return pltpu.make_async_remote_copy(
            src_ref=cells(par, up, half, width - half), dst_ref=relay.at[par, int(up)],
            send_sem=halo_send.at[int(up)], recv_sem=relay_recv.at[par, int(up)],
            device_id=(ax + 4 if up else ax - 4, circ), device_id_type=MESH,
        )

    def from_relay(par, up):
        dst = halo_low if up else halo_high
        return pltpu.make_async_remote_copy(
            src_ref=relay.at[par, int(up)], dst_ref=dst.at[par, :, pl.ds(half, width - half)],
            send_sem=relay_send.at[int(up)], recv_sem=halo_recv.at[par, int(up)],
            device_id=(ax - 3 if up else ax + 3, circ), device_id_type=MESH,
        )

    def start_far(par):
        if corners:
            pl.when(up_far)(to_relay(par, True).start)
            pl.when(down_far)(to_relay(par, False).start)

    def start_ends(par):
        if corners:
            pl.when(up_far)(end_copy(par, True, 0, half).start)
            pl.when(down_far)(end_copy(par, False, 0, half).start)
            pl.when((ax < n_ax - 1) & (turn != 3))(end_copy(par, True, 0, width).start)
            pl.when((ax > 0) & (turn != 0))(end_copy(par, False, 0, width).start)
        else:
            pl.when(ax < n_ax - 1)(end_copy(par, True, 0, width).start)
            pl.when(ax > 0)(end_copy(par, False, 0, width).start)

    def pass_on(par):
        if not corners:
            return
        for up, here in ((True, relay_up), (False, relay_down)):

            @pl.when(here)
            def _():
                to_relay(par, up).wait_recv()
                from_relay(par, up).start()

    def passed_on(par):
        if corners:
            pl.when(relay_up)(from_relay(par, True).wait_send)
            pl.when(relay_down)(from_relay(par, False).wait_send)

    def sides(par):
        to_left = pltpu.make_async_remote_copy(
            src_ref=edge_out.at[0], dst_ref=edge_right.at[par],
            send_sem=edge_send.at[0], recv_sem=edge_recv.at[par, 0],
            device_id=(ax, left), device_id_type=MESH,
        )
        to_right = pltpu.make_async_remote_copy(
            src_ref=edge_out.at[1], dst_ref=edge_left.at[par],
            send_sem=edge_send.at[1], recv_sem=edge_recv.at[par, 1],
            device_id=(ax, right), device_id_type=MESH,
        )
        return to_left, to_right

    def start_sides(par):
        for s in range(3):
            span = pl.ds(s * length, length)
            edge_out[0, span] = musc[par, s, pl.ds(0, length, stride=cycle), :]
            edge_out[1, span] = musc[par, s, pl.ds(cycle - 1, length, stride=cycle), :]
        for copy in sides(par):
            copy.start()

    def local_part(par, nxt, last):
        count = rows // width
        for a in range(count):
            for j in range(0, width, 64):
                here = pl.ds(a * width + j, 64)
                u = [endo[par, s, here, :] for s in range(3)]
                parts = reaction(u[0], u[1], u[2], agonist[here, :])
                for s in range(3):
                    lap = -2.0 * u[s]
                    if a > 0:
                        lap = lap + endo[par, s, pl.ds((a - 1) * width + j, 64), :]
                    if a < count - 1:
                        lap = lap + endo[par, s, pl.ds((a + 1) * width + j, 64), :]
                    value = u[s] + DT * (parts[s] + ENDO_GAP[s] * lap)
                    rhs[s, here, :] = side_by_side(value)

        def musc_base(a, carry):
            here = pl.ds(pl.multiple_of(a * cycle, cycle), cycle)
            place_in = lax.broadcasted_iota(jnp.int32, (cycle, points), 0)
            u = [musc[par, s, here, :] for s in range(3)]
            parts = reaction(u[0], u[1], u[2], None)
            for s in range(3):
                before = jnp.where(place_in == 0, 0.0, pltpu.roll(u[s], 1, 0))
                after = jnp.where(place_in == cycle - 1, 0.0, pltpu.roll(u[s], cycle - 1, 0))
                lap = before + after - 2.0 * u[s]
                value = u[s] + DT * (parts[s] + MUSC_GAP[s] * lap)
                rhs[3 + s, here, :] = side_by_side(value)
            return carry

        lax.fori_loop(0, length, musc_base, 0)
        pass_on(par)

        for layer, state in ((0, endo), (1, musc)):
            for s in range(3):
                value = folded(dot(rhs[layer * 3 + s], weights[layer * 3 + s]))
                state[nxt, s] = value
                if not last:
                    gather(layer, s, value, base_rows)

    def collect(par):
        own_copy(par).wait()
        messages(par).wait_recv()
        for copy in sides(par):
            copy.wait()
        passed_on(par)

        @pl.when(ax > 0)
        def _():
            end_copy(par, False, 0, width).wait_send()
            end_copy(par, True, 0, width).wait_recv()

        @pl.when(ax < n_ax - 1)
        def _():
            end_copy(par, True, 0, width).wait_send()
            end_copy(par, False, 0, width).wait_recv()

    def arrived(par, layer, s):
        flat = recv.at[par].reshape(n * 16, points)
        k = layer * 6 + s * 2
        return jnp.concatenate(
            [flat[pl.ds(k + slot, n, stride=16), :] for slot in range(2)], axis=0
        )

    def endo_outside(par):
        for s in range(3):
            flux = (DT * COUPLING[s]) * (arrived(par, 1, s) - picked[s])
            gap = DT * ENDO_GAP[s]
            value = jnp.concatenate([gap * halo_low[par, s], gap * halo_high[par, s], flux], axis=0)
            block_e[s] = folded(dot(side_by_side(value), weights[s]))

    def musc_outside(par):
        for s in range(3):
            flux = (DT * COUPLING[s]) * (arrived(par, 0, s) - picked[3 + s])
            gap = DT * MUSC_GAP[s]
            span = pl.ds(s * length, length)
            value = jnp.concatenate(
                [gap * edge_left[par, span, :], gap * edge_right[par, span, :], flux], axis=0
            )
            block_m[s] = folded(dot(side_by_side(value), weights[3 + s]))

    def pick():
        for s in range(3):
            picked[s] = base_rows[s] + folded(dot(mix_e[...], side_by_side(block_e[s])))
            picked[3 + s] = base_rows[3 + s] + folded(dot(mix_m[...], side_by_side(block_m[s])))

    def endo_flux():
        flux = jnp.concatenate([block_e[s, pl.ds(2 * width, 2 * n), :] for s in range(3)], axis=1)
        return jnp.concatenate(halves(flux), axis=0)

    def finish_ends(nxt):
        flux = endo_flux()
        for i, first in enumerate((0, rows - width)):
            span = pl.ds(first, width)
            gain = dot(put_e[span, :], flux)
            for s in range(3):
                endo[nxt, s, span, :] += (
                    gain[:, s * points:(s + 1) * points] + block_e[s, pl.ds(i * width, width), :]
                )

    def finish_inside(nxt):
        span = pl.ds(width, rows - 2 * width)
        gain = dot(put_e[span, :], endo_flux())
        for s in range(3):
            endo[nxt, s, span, :] += gain[:, s * points:(s + 1) * points]

    def finish_musc(nxt):
        flux = jnp.concatenate([block_m[s, pl.ds(2 * length, 2 * n), :] for s in range(3)], axis=1)
        gain = dot(put_m[...], jnp.concatenate(halves(flux), axis=0))
        first = pl.ds(0, length, stride=cycle)
        final = pl.ds(cycle - 1, length, stride=cycle)
        for s in range(3):
            musc[nxt, s] += gain[:, s * points:(s + 1) * points]
            musc[nxt, s, first, :] = musc[nxt, s, first, :] + block_m[s, pl.ds(0, length), :]
            musc[nxt, s, final, :] = musc[nxt, s, final, :] + block_m[s, pl.ds(length, length), :]

    start_far(0)
    pack(0)
    launch(0)
    start_ends(0)
    start_sides(0)

    def step(t, carry):
        par = lax.rem(t, 2)
        nxt = 1 - par
        local_part(par, nxt, False)
        collect(par)
        endo_outside(par)
        finish_ends(nxt)
        start_far(nxt)
        musc_outside(par)
        pick()
        pl.when(t > 0)(lambda: messages(nxt).wait_send())
        pack(nxt)
        launch(nxt)
        start_ends(nxt)
        finish_musc(nxt)
        start_sides(nxt)
        finish_inside(nxt)
        return carry

    lax.fori_loop(0, TIME_STEPS - 1, step, 0)
    par = (TIME_STEPS - 1) % 2
    nxt = 1 - par
    local_part(par, nxt, True)
    collect(par)
    endo_outside(par)
    finish_ends(nxt)
    finish_inside(nxt)
    store_e = pltpu.make_async_copy(endo.at[nxt], endo_out, in_sems.at[0])
    store_e.start()
    musc_outside(par)
    finish_musc(nxt)
    store_m = pltpu.make_async_copy(musc.at[nxt], musc_out, in_sems.at[1])
    store_m.start()
    messages(nxt).wait_send()
    messages(par).wait_send()
    store_e.wait()
    store_m.wait()


def hand_over(endo_from, musc_from, endo_to, musc_to, endo, musc, sems, out_sems):
    pairs = []
    for layer, (a, held, b) in enumerate(((endo_from, endo, endo_to), (musc_from, musc, musc_to))):
        for s in range(held.shape[0]):
            pairs.append((
                pltpu.make_async_copy(a.at[s], held.at[s], sems.at[layer, s]),
                pltpu.make_async_copy(held.at[s], b.at[s], out_sems.at[layer, s]),
            ))
    for load, store in pairs:
        load.start()
    for load, store in pairs:
        load.wait()
        store.start()
    for load, store in pairs:
        store.wait()


def local(
    n_ax, n_circ,
    endothelium, muscle, agonist, proj_cell, proj_target, proj_count, endo_inverse, muscle_inverse
):
    n = n_ax * n_circ
    species, endo_ax, width, points = endothelium.shape
    length, cycle = muscle.shape[1:3]
    rows = endo_ax * width
    musc_rows = length * cycle
    slots = proj_cell.shape[2]
    anywhere = pl.BlockSpec(memory_space=pl.ANY)
    dma = pltpu.SemaphoreType.DMA
    body = functools.partial(kernel, (n_ax, n_circ, width, length, cycle))
    endo_next, musc_next = pl.pallas_call(
        body,
        out_shape=(
            jax.ShapeDtypeStruct((species, rows, points), F32),
            jax.ShapeDtypeStruct((species, musc_rows, points), F32),
        ),
        in_specs=[anywhere] * 8,
        out_specs=(anywhere, anywhere),
        scratch_shapes=[
            pltpu.VMEM((2, species, rows, points), F32),
            pltpu.VMEM((2, species, musc_rows, points), F32),
            pltpu.VMEM((2, species, width, points), F32),
            pltpu.VMEM((2, species, width, points), F32),
            pltpu.VMEM((2, species * length, points), F32),
            pltpu.VMEM((2, species * length, points), F32),
            pltpu.VMEM((2, species * length, points), F32),
            pltpu.VMEM((2, n, 16, points), F32),
            pltpu.VMEM((2, n, 16, points), F32),
            pltpu.VMEM((6, slots * n, points), F32),
            pltpu.VMEM((6, slots * n, points), F32),
            pltpu.VMEM((6, 2 * points, 2 * points), BF16),
            pltpu.VMEM((slots * n, rows), BF16),
            pltpu.VMEM((slots * n, musc_rows), BF16),
            pltpu.VMEM((rows, 2 * slots * n), BF16),
            pltpu.VMEM((musc_rows, 2 * slots * n), BF16),
            pltpu.VMEM((slots * n, 2 * width + slots * n), BF16),
            pltpu.VMEM((slots * n, 2 * length + slots * n), BF16),
            pltpu.VMEM((6, max(rows, musc_rows), 2 * points), BF16),
            pltpu.VMEM((species, 2 * width + slots * n, points), F32),
            pltpu.VMEM((species, 2 * length + slots * n, points), F32),
            pltpu.VMEM((rows, points), F32),
            pltpu.VMEM((n, 1, points), jnp.int32),
            pltpu.VMEM((n, 1, points), jnp.int32),
            pltpu.VMEM((species, points, points), F32),
            pltpu.VMEM((species, points, points), F32),
            pltpu.VMEM((slots, n), jnp.int32),
            pltpu.VMEM((slots, n), jnp.int32),
            pltpu.VMEM((1, n), jnp.int32),
            dma((8,)), dma, dma((2,)), dma((2,)),
            dma((2,)), dma((2, 2)), dma((2,)), dma((2, 2)),
            dma((2,)),
            pltpu.VMEM((2, 2, species, width - width // 2, points), F32),
            dma((2, 2)), dma((2,)),
        ],
        compiler_params=pltpu.CompilerParams(
            collective_id=0, has_side_effects=True, vmem_limit_bytes=60 * 1024 * 1024
        ),
        name="cable_steps",
    )(
        endothelium.reshape(species, rows, points),
        muscle.reshape(species, musc_rows, points),
        agonist.reshape(rows, points),
        proj_target[0].T, proj_cell[0].T, proj_count,
        endo_inverse, muscle_inverse,
    )
    endo_next, musc_next = pl.pallas_call(
        hand_over,
        out_shape=(
            jax.ShapeDtypeStruct((species, rows, points), F32),
            jax.ShapeDtypeStruct((species, musc_rows, points), F32),
        ),
        in_specs=[anywhere] * 2,
        out_specs=(anywhere, anywhere),
        scratch_shapes=[
            pltpu.VMEM((species, rows, points), F32),
            pltpu.VMEM((species, musc_rows, points), F32),
            dma((2, species)), dma((2, species)),
        ],
        compiler_params=pltpu.CompilerParams(vmem_limit_bytes=60 * 1024 * 1024),
        name="hand_over",
    )(endo_next, musc_next)
    return endo_next.reshape(endothelium.shape), musc_next.reshape(muscle.shape)


def solution(mesh):
    tiles = P(None, "ax", "circ", None)
    sent = P(("ax", "circ"), None, None)
    return jax.shard_map(
        functools.partial(local, mesh.shape["ax"], mesh.shape["circ"]),
        mesh=mesh,
        in_specs=(tiles, tiles, P("ax", "circ", None), sent, sent, P(("ax", "circ"), None), P(), P()),
        out_specs=(tiles, tiles),
        check_vma=False,
    )
```

```python
import functools

import jax
import jax.numpy as jnp
from jax import lax
from jax.experimental import pallas as pl
from jax.experimental.pallas import tpu as pltpu
from jax.sharding import PartitionSpec as P

MESH = pl.DeviceIdType.MESH
TIME_STEPS = 8
DT = 0.2
COUPLING = (0.1, 0.3, 0.5)
ENDO_GAP = (0.05, 0.3, 0.5)
MUSC_GAP = (0.05, 0.1, 0.4)
BF16 = jnp.bfloat16
F32 = jnp.float32


def halves(x):
    high = x.astype(BF16)
    return high, (x - high.astype(F32)).astype(BF16)


def side_by_side(x):
    return jnp.concatenate(halves(x), axis=1)


def folded(y):
    half = y.shape[1] // 2
    return y[:, :half] + y[:, half:]


def dot(a, b):
    return jnp.dot(a, b, preferred_element_type=F32)


def reaction(u0, u1, u2, drive):
    square = u1 * u1
    release = square / (0.5 + square)
    second = -0.5 * u1 if drive is None else drive - 0.5 * u1
    return (1.2 * release - 0.6 * u0 - 0.2 * u2, second, 0.5 * u0 - 0.8 * u2)


def kernel(
    sizes,
    endo_in, musc_in, agonist_in, target_in, cell_in, count_in, endo_inv_in, musc_inv_in,
    endo_out, musc_out,
    endo, musc, halo_low, halo_high, edge_out, edge_left, edge_right,
    send, recv, picked, base_rows, weights, take_e, take_m, put_e, put_m, mix_e, mix_m, rhs,
    block_e, block_m, agonist, meta, meta_recv, endo_inv, musc_inv, targets, starts_at, counts,
    in_sems, own_sem, send_sem, recv_sem, halo_send, halo_recv, edge_send, edge_recv,
    meta_sems, relay, relay_recv, relay_send,
):
    n_ax, n_circ, width, length, cycle = sizes
    n = n_ax * n_circ
    points = endo.shape[3]
    rows = endo.shape[2]
    musc_rows = musc.shape[2]
    ax = lax.axis_index("ax")
    circ = lax.axis_index("circ")
    me = ax * n_circ + circ
    right = lax.rem(circ + 1, n_circ)
    left = lax.rem(circ + n_circ - 1, n_circ)
    half = width // 2
    corners = n_ax % 4 == 0 and n_ax > 4
    turn = lax.rem(ax, 4)
    up_far = (turn == 3) & (ax < n_ax - 1)
    down_far = (turn == 0) & (ax > 0)
    relay_up = (turn == 3) & (ax > 3)
    relay_down = (turn == 0) & (ax < n_ax - 4)
    turned = [lax.rem(circ + c, n_circ) for c in range(n_circ)]

    def each_peer(act):
        def some(j, carry):
            far = lax.rem(ax + j, n_ax)
            for c in reversed(range(n_circ)):
                act(far, turned[c])
            return carry

        lax.fori_loop(1, n_ax, some, 0)
        for c in reversed(range(1, n_circ)):
            act(ax, turned[c])

    loads = [
        pltpu.make_async_copy(a, b, in_sems.at[i])
        for i, (a, b) in enumerate(
            (
                (target_in, targets), (endo_in, endo.at[0]), (musc_in, musc.at[0]),
                (endo_inv_in, endo_inv), (musc_inv_in, musc_inv), (agonist_in, agonist),
                (cell_in, starts_at), (count_in, counts),
            )
        )
    ]
    for load in loads:
        load.start()

    barrier = pltpu.get_barrier_semaphore()

    def greet(pa, pc):
        pl.semaphore_signal(barrier, inc=1, device_id=(pa, pc), device_id_type=MESH)

    each_peer(greet)

    @pl.when(ax == 0)
    def _():
        halo_low[...] = jnp.zeros_like(halo_low)

    @pl.when(ax == n_ax - 1)
    def _():
        halo_high[...] = jnp.zeros_like(halo_high)

    for i in (0, 6, 7):
        loads[i].wait()
    live = lax.broadcasted_iota(jnp.int32, targets.shape, 0) < counts[...]
    nowhere = rows + musc_rows
    table = jnp.concatenate(
        [
            jnp.where(live, targets[...], nowhere).astype(F32),
            jnp.where(live, starts_at[...], nowhere).astype(F32),
            jnp.zeros((4, n), F32),
        ],
        axis=0,
    )
    if n % 128:
        table = jnp.concatenate([table, jnp.zeros((8, 128 - n % 128), F32)], axis=1)
    columns = table.T[:n]
    meta[:, 0, :] = jnp.concatenate(
        [columns, jnp.zeros((n, points - 8), F32)], axis=1
    ).astype(jnp.int32)
    pl.semaphore_wait(barrier, n - 1)

    def tell(pa, pc):
        pltpu.make_async_remote_copy(
            src_ref=meta.at[pa * n_circ + pc], dst_ref=meta_recv.at[me],
            send_sem=meta_sems.at[0], recv_sem=meta_sems.at[1],
            device_id=(pa, pc), device_id_type=MESH,
        ).start()

    each_peer(tell)
    own_meta = pltpu.make_async_copy(meta.at[me], meta_recv.at[me], own_sem)
    own_meta.start()

    loads[3].wait()
    loads[4].wait()
    for layer, inv in ((0, endo_inv), (1, musc_inv)):
        for s in range(3):
            row = side_by_side(inv[s].T)
            weights[layer * 3 + s] = jnp.concatenate([row, row], axis=0)

    def choose(ids, take, put):
        cells = lax.broadcasted_iota(jnp.int32, take.shape, 1)
        chosen = jnp.where(cells == ids, 1.0, 0.0)
        take[...] = chosen.astype(BF16)
        spread = chosen.T
        put[...] = jnp.concatenate([spread, spread], axis=1).astype(BF16)
        return chosen, dot(chosen.astype(BF16), spread.astype(BF16))

    sent = meta[:, 0, :]
    ids = jnp.concatenate([sent[:, 2:3], sent[:, 3:4]], axis=0)
    chosen, same = choose(ids, take_e, put_e)
    mix_e[...] = jnp.concatenate(
        [chosen[:, :width], chosen[:, rows - width:], same], axis=1
    ).astype(BF16)

    def gather(layer, s, values, out):
        take = take_e if layer == 0 else take_m
        out[layer * 3 + s] = folded(dot(take[...], side_by_side(values)))

    loads[1].wait()
    loads[2].wait()
    loads[5].wait()
    for s in range(3):
        gather(0, s, endo[0, s], picked)

    told = pltpu.make_async_remote_copy(
        src_ref=meta.at[pl.ds(0, n - 1)], dst_ref=meta_recv.at[pl.ds(0, n - 1)],
        send_sem=meta_sems.at[0], recv_sem=meta_sems.at[1],
        device_id=(ax, right), device_id_type=MESH,
    )
    told.wait_recv()
    own_meta.wait()
    got = meta_recv[:, 0, :]
    ids = jnp.concatenate([got[:, 0:1], got[:, 1:2]], axis=0)
    chosen, same = choose(ids, take_m, put_m)
    starts = lax.broadcasted_iota(jnp.int32, (ids.shape[0], length), 1) * cycle
    mix_m[...] = jnp.concatenate(
        [
            jnp.where(starts == ids, 1.0, 0.0),
            jnp.where(starts + (cycle - 1) == ids, 1.0, 0.0),
            same,
        ],
        axis=1,
    ).astype(BF16)
    for s in range(3):
        gather(1, s, musc[0, s], picked)
    told.wait_send()

    def messages(par):
        return pltpu.make_async_remote_copy(
            src_ref=send.at[par, pl.ds(0, n - 1), pl.ds(0, 12)],
            dst_ref=recv.at[par, pl.ds(0, n - 1), pl.ds(0, 12)],
            send_sem=send_sem.at[par], recv_sem=recv_sem.at[par],
            device_id=(ax, right), device_id_type=MESH,
        )

    def own_copy(par):
        return pltpu.make_async_copy(
            send.at[par, me, pl.ds(0, 12)], recv.at[par, me, pl.ds(0, 12)], own_sem
        )

    def pack(par):
        flat = send.at[par].reshape(n * 16, points)
        for q in range(6):
            for slot in range(2):
                flat[pl.ds(q * 2 + slot, n, stride=16), :] = picked[q, pl.ds(slot * n, n), :]

    def launch(par):
        def post(pa, pc):
            pltpu.make_async_remote_copy(
                src_ref=send.at[par, pa * n_circ + pc, pl.ds(0, 12)],
                dst_ref=recv.at[par, me, pl.ds(0, 12)],
                send_sem=send_sem.at[par],
                recv_sem=recv_sem.at[par],
                device_id=(pa, pc),
                device_id_type=MESH,
            ).start()

        each_peer(post)
        own_copy(par).start()

    def cells(par, from_top, start, count):
        first = rows - width if from_top else 0
        return endo.at[par, :, pl.ds(first + start, count)]

    def end_copy(par, up, start, count):
        dst = halo_low if up else halo_high
        return pltpu.make_async_remote_copy(
            src_ref=cells(par, up, start, count), dst_ref=dst.at[par, :, pl.ds(start, count)],
            send_sem=halo_send.at[int(up)], recv_sem=halo_recv.at[par, int(up)],
            device_id=(ax + 1 if up else ax - 1, circ), device_id_type=MESH,
        )

    def to_relay(par, up):
        return pltpu.make_async_remote_copy(
            src_ref=cells(par, up, half, width - half), dst_ref=relay.at[par, int(up)],
            send_sem=halo_send.at[int(up)], recv_sem=relay_recv.at[par, int(up)],
            device_id=(ax + 4 if up else ax - 4, circ), device_id_type=MESH,
        )

    def from_relay(par, up):
        dst = halo_low if up else halo_high
        return pltpu.make_async_remote_copy(
            src_ref=relay.at[par, int(up)], dst_ref=dst.at[par, :, pl.ds(half, width - half)],
            send_sem=relay_send.at[int(up)], recv_sem=halo_recv.at[par, int(up)],
            device_id=(ax - 3 if up else ax + 3, circ), device_id_type=MESH,
        )

    def start_far(par):
        if corners:
            pl.when(up_far)(to_relay(par, True).start)
            pl.when(down_far)(to_relay(par, False).start)

    def start_ends(par):
        if corners:
            pl.when(up_far)(end_copy(par, True, 0, half).start)
            pl.when(down_far)(end_copy(par, False, 0, half).start)
            pl.when((ax < n_ax - 1) & (turn != 3))(end_copy(par, True, 0, width).start)
            pl.when((ax > 0) & (turn != 0))(end_copy(par, False, 0, width).start)
        else:
            pl.when(ax < n_ax - 1)(end_copy(par, True, 0, width).start)
            pl.when(ax > 0)(end_copy(par, False, 0, width).start)

    def pass_on(par):
        if not corners:
            return
        for up, here in ((True, relay_up), (False, relay_down)):

            @pl.when(here)
            def _():
                to_relay(par, up).wait_recv()
                from_relay(par, up).start()

    def passed_on(par):
        if corners:
            pl.when(relay_up)(from_relay(par, True).wait_send)
            pl.when(relay_down)(from_relay(par, False).wait_send)

    def sides(par):
        to_left = pltpu.make_async_remote_copy(
            src_ref=edge_out.at[0], dst_ref=edge_right.at[par],
            send_sem=edge_send.at[0], recv_sem=edge_recv.at[par, 0],
            device_id=(ax, left), device_id_type=MESH,
        )
        to_right = pltpu.make_async_remote_copy(
            src_ref=edge_out.at[1], dst_ref=edge_left.at[par],
            send_sem=edge_send.at[1], recv_sem=edge_recv.at[par, 1],
            device_id=(ax, right), device_id_type=MESH,
        )
        return to_left, to_right

    def start_sides(par):
        for s in range(3):
            span = pl.ds(s * length, length)
            edge_out[0, span] = musc[par, s, pl.ds(0, length, stride=cycle), :]
            edge_out[1, span] = musc[par, s, pl.ds(cycle - 1, length, stride=cycle), :]
        for copy in sides(par):
            copy.start()

    def local_part(par, nxt, last):
        count = rows // width
        for a in range(count):
            for j in range(0, width, 64):
                here = pl.ds(a * width + j, 64)
                u = [endo[par, s, here, :] for s in range(3)]
                parts = reaction(u[0], u[1], u[2], agonist[here, :])
                for s in range(3):
                    lap = -2.0 * u[s]
                    if a > 0:
                        lap = lap + endo[par, s, pl.ds((a - 1) * width + j, 64), :]
                    if a < count - 1:
                        lap = lap + endo[par, s, pl.ds((a + 1) * width + j, 64), :]
                    value = u[s] + DT * (parts[s] + ENDO_GAP[s] * lap)
                    rhs[s, here, :] = side_by_side(value)

        def musc_base(a, carry):
            here = pl.ds(pl.multiple_of(a * cycle, cycle), cycle)
            place_in = lax.broadcasted_iota(jnp.int32, (cycle, points), 0)
            u = [musc[par, s, here, :] for s in range(3)]
            parts = reaction(u[0], u[1], u[2], None)
            for s in range(3):
                before = jnp.where(place_in == 0, 0.0, pltpu.roll(u[s], 1, 0))
                after = jnp.where(place_in == cycle - 1, 0.0, pltpu.roll(u[s], cycle - 1, 0))
                lap = before + after - 2.0 * u[s]
                value = u[s] + DT * (parts[s] + MUSC_GAP[s] * lap)
                rhs[3 + s, here, :] = side_by_side(value)
            return carry

        lax.fori_loop(0, length, musc_base, 0)
        pass_on(par)

        for layer, state in ((0, endo), (1, musc)):
            for s in range(3):
                value = folded(dot(rhs[layer * 3 + s], weights[layer * 3 + s]))
                state[nxt, s] = value
                if not last:
                    gather(layer, s, value, base_rows)

    def collect(par):
        own_copy(par).wait()
        messages(par).wait_recv()
        for copy in sides(par):
            copy.wait()
        passed_on(par)

        @pl.when(ax > 0)
        def _():
            end_copy(par, False, 0, width).wait_send()
            end_copy(par, True, 0, width).wait_recv()

        @pl.when(ax < n_ax - 1)
        def _():
            end_copy(par, True, 0, width).wait_send()
            end_copy(par, False, 0, width).wait_recv()

    def arrived(par, layer, s):
        flat = recv.at[par].reshape(n * 16, points)
        k = layer * 6 + s * 2
        return jnp.concatenate(
            [flat[pl.ds(k + slot, n, stride=16), :] for slot in range(2)], axis=0
        )

    def endo_outside(par):
        for s in range(3):
            flux = (DT * COUPLING[s]) * (arrived(par, 1, s) - picked[s])
            gap = DT * ENDO_GAP[s]
            value = jnp.concatenate([gap * halo_low[par, s], gap * halo_high[par, s], flux], axis=0)
            block_e[s] = folded(dot(side_by_side(value), weights[s]))

    def musc_outside(par):
        for s in range(3):
            flux = (DT * COUPLING[s]) * (arrived(par, 0, s) - picked[3 + s])
            gap = DT * MUSC_GAP[s]
            span = pl.ds(s * length, length)
            value = jnp.concatenate(
                [gap * edge_left[par, span, :], gap * edge_right[par, span, :], flux], axis=0
            )
            block_m[s] = folded(dot(side_by_side(value), weights[3 + s]))

    def pick():
        for s in range(3):
            picked[s] = base_rows[s] + folded(dot(mix_e[...], side_by_side(block_e[s])))
            picked[3 + s] = base_rows[3 + s] + folded(dot(mix_m[...], side_by_side(block_m[s])))

    def endo_flux():
        flux = jnp.concatenate([block_e[s, pl.ds(2 * width, 2 * n), :] for s in range(3)], axis=1)
        return jnp.concatenate(halves(flux), axis=0)

    def finish_ends(nxt):
        flux = endo_flux()
        for i, first in enumerate((0, rows - width)):
            span = pl.ds(first, width)
            gain = dot(put_e[span, :], flux)
            for s in range(3):
                endo[nxt, s, span, :] += (
                    gain[:, s * points:(s + 1) * points] + block_e[s, pl.ds(i * width, width), :]
                )

    def finish_inside(nxt):
        span = pl.ds(width, rows - 2 * width)
        gain = dot(put_e[span, :], endo_flux())
        for s in range(3):
            endo[nxt, s, span, :] += gain[:, s * points:(s + 1) * points]

    def finish_musc(nxt):
        flux = jnp.concatenate([block_m[s, pl.ds(2 * length, 2 * n), :] for s in range(3)], axis=1)
        gain = dot(put_m[...], jnp.concatenate(halves(flux), axis=0))
        first = pl.ds(0, length, stride=cycle)
        final = pl.ds(cycle - 1, length, stride=cycle)
        for s in range(3):
            musc[nxt, s] += gain[:, s * points:(s + 1) * points]
            musc[nxt, s, first, :] = musc[nxt, s, first, :] + block_m[s, pl.ds(0, length), :]
            musc[nxt, s, final, :] = musc[nxt, s, final, :] + block_m[s, pl.ds(length, length), :]

    start_far(0)
    pack(0)
    launch(0)
    start_ends(0)
    start_sides(0)

    def step(t, carry):
        par = lax.rem(t, 2)
        nxt = 1 - par
        local_part(par, nxt, False)
        pl.when(t > 0)(lambda: messages(nxt).wait_send())
        collect(par)
        endo_outside(par)
        musc_outside(par)
        pick()
        pack(nxt)
        finish_ends(nxt)
        start_far(nxt)
        launch(nxt)
        start_ends(nxt)
        finish_musc(nxt)
        start_sides(nxt)
        finish_inside(nxt)
        return carry

    lax.fori_loop(0, TIME_STEPS - 1, step, 0)
    par = (TIME_STEPS - 1) % 2
    nxt = 1 - par
    local_part(par, nxt, True)
    collect(par)
    endo_outside(par)
    finish_ends(nxt)
    finish_inside(nxt)
    store_e = pltpu.make_async_copy(endo.at[nxt], endo_out, in_sems.at[0])
    store_e.start()
    musc_outside(par)
    finish_musc(nxt)
    store_m = pltpu.make_async_copy(musc.at[nxt], musc_out, in_sems.at[1])
    store_m.start()
    messages(nxt).wait_send()
    messages(par).wait_send()
    store_e.wait()
    store_m.wait()


def hand_over(endo_from, musc_from, endo_to, musc_to, endo, musc, sems, out_sems):
    pairs = []
    for layer, (a, held, b) in enumerate(((endo_from, endo, endo_to), (musc_from, musc, musc_to))):
        for s in range(held.shape[0]):
            pairs.append((
                pltpu.make_async_copy(a.at[s], held.at[s], sems.at[layer, s]),
                pltpu.make_async_copy(held.at[s], b.at[s], out_sems.at[layer, s]),
            ))
    for load, store in pairs:
        load.start()
    for load, store in pairs:
        load.wait()
        store.start()
    for load, store in pairs:
        store.wait()


def local(
    n_ax, n_circ,
    endothelium, muscle, agonist, proj_cell, proj_target, proj_count, endo_inverse, muscle_inverse
):
    n = n_ax * n_circ
    species, endo_ax, width, points = endothelium.shape
    length, cycle = muscle.shape[1:3]
    rows = endo_ax * width
    musc_rows = length * cycle
    slots = proj_cell.shape[2]
    anywhere = pl.BlockSpec(memory_space=pl.ANY)
    dma = pltpu.SemaphoreType.DMA
    body = functools.partial(kernel, (n_ax, n_circ, width, length, cycle))
    endo_next, musc_next = pl.pallas_call(
        body,
        out_shape=(
            jax.ShapeDtypeStruct((species, rows, points), F32),
            jax.ShapeDtypeStruct((species, musc_rows, points), F32),
        ),
        in_specs=[anywhere] * 8,
        out_specs=(anywhere, anywhere),
        scratch_shapes=[
            pltpu.VMEM((2, species, rows, points), F32),
            pltpu.VMEM((2, species, musc_rows, points), F32),
            pltpu.VMEM((2, species, width, points), F32),
            pltpu.VMEM((2, species, width, points), F32),
            pltpu.VMEM((2, species * length, points), F32),
            pltpu.VMEM((2, species * length, points), F32),
            pltpu.VMEM((2, species * length, points), F32),
            pltpu.VMEM((2, n, 16, points), F32),
            pltpu.VMEM((2, n, 16, points), F32),
            pltpu.VMEM((6, slots * n, points), F32),
            pltpu.VMEM((6, slots * n, points), F32),
            pltpu.VMEM((6, 2 * points, 2 * points), BF16),
            pltpu.VMEM((slots * n, rows), BF16),
            pltpu.VMEM((slots * n, musc_rows), BF16),
            pltpu.VMEM((rows, 2 * slots * n), BF16),
            pltpu.VMEM((musc_rows, 2 * slots * n), BF16),
            pltpu.VMEM((slots * n, 2 * width + slots * n), BF16),
            pltpu.VMEM((slots * n, 2 * length + slots * n), BF16),
            pltpu.VMEM((6, max(rows, musc_rows), 2 * points), BF16),
            pltpu.VMEM((species, 2 * width + slots * n, points), F32),
            pltpu.VMEM((species, 2 * length + slots * n, points), F32),
            pltpu.VMEM((rows, points), F32),
            pltpu.VMEM((n, 1, points), jnp.int32),
            pltpu.VMEM((n, 1, points), jnp.int32),
            pltpu.VMEM((species, points, points), F32),
            pltpu.VMEM((species, points, points), F32),
            pltpu.VMEM((slots, n), jnp.int32),
            pltpu.VMEM((slots, n), jnp.int32),
            pltpu.VMEM((1, n), jnp.int32),
            dma((8,)), dma, dma((2,)), dma((2,)),
            dma((2,)), dma((2, 2)), dma((2,)), dma((2, 2)),
            dma((2,)),
            pltpu.VMEM((2, 2, species, width - width // 2, points), F32),
            dma((2, 2)), dma((2,)),
        ],
        compiler_params=pltpu.CompilerParams(
            collective_id=0, has_side_effects=True, vmem_limit_bytes=60 * 1024 * 1024
        ),
        name="cable_steps",
    )(
        endothelium.reshape(species, rows, points),
        muscle.reshape(species, musc_rows, points),
        agonist.reshape(rows, points),
        proj_target[0].T, proj_cell[0].T, proj_count,
        endo_inverse, muscle_inverse,
    )
    endo_next, musc_next = pl.pallas_call(
        hand_over,
        out_shape=(
            jax.ShapeDtypeStruct((species, rows, points), F32),
            jax.ShapeDtypeStruct((species, musc_rows, points), F32),
        ),
        in_specs=[anywhere] * 2,
        out_specs=(anywhere, anywhere),
        scratch_shapes=[
            pltpu.VMEM((species, rows, points), F32),
            pltpu.VMEM((species, musc_rows, points), F32),
            dma((2, species)), dma((2, species)),
        ],
        compiler_params=pltpu.CompilerParams(vmem_limit_bytes=60 * 1024 * 1024),
        name="hand_over",
    )(endo_next, musc_next)
    return endo_next.reshape(endothelium.shape), musc_next.reshape(muscle.shape)


def solution(mesh):
    tiles = P(None, "ax", "circ", None)
    sent = P(("ax", "circ"), None, None)
    return jax.shard_map(
        functools.partial(local, mesh.shape["ax"], mesh.shape["circ"]),
        mesh=mesh,
        in_specs=(tiles, tiles, P("ax", "circ", None), sent, sent, P(("ax", "circ"), None), P(), P()),
        out_specs=(tiles, tiles),
        check_vma=False,
    )
```
